256 devices in a mesh: grp: 8 (over z_hi, core), tile: 32 (over x, y, z_lo).
Axes of the slice: x: 4, y: 4, z: 8 (z_hi: 4, z_lo: 2; z = z_hi * 2 + z_lo), core: 2. Of those that a mesh axis runs over, the one named last changes fastest.
Arguments:
- right_side: float32 [256, 16384], P('grp', 'tile'), may hold values from -8 to 8
- diagonal: float32 [256, 16384], P('grp', 'tile'), may hold values from 0.25 to 2
- inverse_factor: float32 [16384, 16384], P(('grp', 'tile')), may hold values from -2 to 2, as said below
Outputs:
- solution_field: float32 [256, 16384], P('grp', 'tile')
The draws below stay inside these ranges and needn't reach their ends.
Inputs may be any that keep to these rules, and one draw needn't show every extreme that they name: `inverse_factor`: zero above the diagonal; the diagonal lies between 1 and 2.
All inputs are finite; a program needn't handle non-finite values.
Results may differ from the reference program's by a relative error of at most 0.0003.
Values sent between devices are 32-bit elements; how exact they have to be, the bound alone decides.
A program may use at most 64 MiB of HBM per device.

```python
import jax
import jax.numpy as jnp
from jax import lax

RD = 32
CD = 512
FAC = 16
SWEEPS = 4
CYCLES = 2
NCO = 16384
NR = 256
NC = 16384
N_GRP = 8
N_TILE = 32


def draw_inverse_factor(key, part):
    key_diag = jax.random.fold_in(key, 11)
    key_off = jax.random.fold_in(key, 23)
    diag_vals = jax.random.uniform(key_diag, (NCO,), jnp.float32, 1.0, 2.0)
    off = jax.random.normal(key_off, (NCO, NCO), jnp.float32) * (0.4 / jnp.sqrt(NCO * 1.0))
    off = jnp.clip(jnp.tril(off, -1), -0.9, 0.9)
    return off + jnp.diag(diag_vals)


def block_scale(stream_key, dims, pieces, low, top_value):
    loudness, own = 1.0, jax.random.fold_in(stream_key, 6)
    for position, parts in pieces:
        draws = jnp.exp(jax.random.uniform(jax.random.fold_in(own, position), (parts,), jnp.float32, low / len(pieces), top_value / len(pieces)))
        loudness = loudness * jnp.repeat(draws, dims[position] // parts).reshape([-1 if axis == position else 1 for axis in range(len(dims))])
    return loudness


def scatter_about(key, dims, scale, reach, shards=(), kind=jnp.bfloat16):
    result = scale * jax.random.normal(key, dims, jnp.float32)
    if shards:
        result = result * block_scale(key, dims, shards, -0.22, 0.18)
    return jnp.clip(result, -reach, reach).astype(kind)


def setup_inputs(seed: int = 0) -> dict:
    keys = jax.random.split(jax.random.key(seed), 4)
    right_side = scatter_about(keys[0], (NR, NC), 1.0, 8.0, ((0, 8), (1, 32)), jnp.float32)
    diagonal = jnp.clip(0.25 + 1.75 * jax.random.uniform(keys[1], (NR, NC), jnp.float32) ** block_scale(keys[1], (NR, NC), ((0, 8), (1, 32)), -0.2, 0.2), 0.25, 2.0)
    inverse_factor = draw_inverse_factor(jax.random.fold_in(keys[3], 71), 0)
    return dict(right_side=right_side, diagonal=diagonal, inverse_factor=inverse_factor)


def operate(field, diagonal):
    padded = jnp.pad(field, 1)
    beside = padded[2:, 1:-1] + padded[:-2, 1:-1] + padded[1:-1, 2:] + padded[1:-1, :-2]
    beside = beside + padded[2:, :-2] + padded[:-2, 2:]
    return (6.0 + diagonal) * field - beside


def restrict(field):
    blocks = field.reshape(N_GRP, RD // FAC, FAC, N_TILE, CD // FAC, FAC)
    means = jnp.mean(blocks, axis=(2, 5))
    return jnp.transpose(means, (0, 2, 1, 3)).reshape(-1)


def prolong(values):
    blocks = values.reshape(N_GRP, N_TILE, RD // FAC, CD // FAC)
    blocks = jnp.transpose(blocks, (0, 2, 1, 3))
    blocks = jnp.repeat(jnp.repeat(blocks, FAC, axis=1), FAC, axis=3)
    return blocks.reshape(N_GRP * RD, N_TILE * CD)


def reference(right_side, diagonal, inverse_factor):
    scale = 1.0 / (6.0 + diagonal)
    solution_field = jnp.zeros_like(right_side)
    for cycle in range(CYCLES):
        residual = right_side - operate(solution_field, diagonal)
        smoothed = 0.8 * residual * scale
        for sweep in range(SWEEPS - 1):
            smoothed = smoothed + 0.8 * (residual - operate(smoothed, diagonal)) * scale
        coarse_rhs = restrict(residual)
        inner = jnp.dot(inverse_factor, coarse_rhs, precision=lax.Precision.HIGHEST)
        coarse_fix = jnp.dot(inner, inverse_factor, precision=lax.Precision.HIGHEST)
        solution_field = solution_field + smoothed + 0.5 * prolong(coarse_fix)
    return solution_field
```

```python
import functools

import jax
import jax.numpy as jnp
from jax import lax
from jax.experimental import pallas as pl
from jax.experimental.pallas import tpu as pltpu
from jax.sharding import PartitionSpec as P

MESH = pl.DeviceIdType.MESH
HIGHEST = lax.Precision.HIGHEST
RD, CD, FAC = 32, 512, 16
N_GRP, N_TILE = 8, 32
HR, HC = 8, 128
ER, EC = RD + 2 * HR, CD + 2 * HC
CO = 64
N_LANE, N_Z = 32, 8
DIRECTIONS = [(a, b) for a in (-1, 0, 1) for b in (-1, 0, 1) if (a, b) != (0, 0)]


def device_at(m, z):
    return ((z // 2) * 2 + m // 16, (m % 16) * 2 + z % 2)


def beside(field):
    right = pltpu.roll(field, EC - 1, 1)
    left = pltpu.roll(field, 1, 1)
    return right + left + pltpu.roll(field + right, 1, 0) + pltpu.roll(field + left, ER - 1, 0)


def lanes(shape):
    return lax.broadcasted_iota(jnp.int32, shape, len(shape) - 1)


def restricted(block, z_lo):
    top = jnp.sum(block[:FAC], axis=0, keepdims=True)
    low = jnp.sum(block[FAC:], axis=0, keepdims=True)
    sums = jnp.concatenate([top, low, jnp.zeros((6, CD), jnp.float32)], axis=0)
    cell = lax.broadcasted_iota(jnp.int32, (CD, 128), 0) // FAC
    gather = jnp.where(cell == lanes((CD, 128)) % 32, 1.0 / (FAC * FAC), 0.0).astype(jnp.float32)
    means = jnp.dot(sums, gather, precision=HIGHEST, preferred_element_type=jnp.float32)
    lane = lanes((1, 128))
    row = jnp.where((lane // 32) % 2 == 0, means[0:1], means[1:2])
    return jnp.where(lane // 64 == z_lo, row, 0.0)


def spread_columns(rows):
    cell = lax.broadcasted_iota(jnp.int32, (128, CD), 0) % 32
    spread = jnp.where(cell == lanes((128, CD)) // FAC, 1.0, 0.0).astype(jnp.float32)
    return jnp.dot(rows, spread, precision=HIGHEST, preferred_element_type=jnp.float32)


def quarter(row, z_lo, i_hi, valid):
    lane = lanes((1, 128))
    keep = (lane // 32 == z_lo * 2 + i_hi) & valid
    return jnp.where(keep, row, 0.0)


def coarse_neighbours(field):
    sub = lax.broadcasted_iota(jnp.int32, (8, 128), 0)
    lane = lanes((8, 128))
    second = (lane // 32) % 2 == 1
    edge_hi, edge_lo = lane % 32 == 31, lane % 32 == 0
    z_hi_half = lane // 64 == 1
    straight, to_right, to_left = [], [], []
    for c in field:
        fwd = pltpu.roll(c, 32, 1)
        back = pltpu.roll(c, 96, 1)
        above = jnp.where(sub >= 4, pltpu.roll(back, 4, 0), pltpu.roll(back, 5, 0))
        above = jnp.where(sub == 0, 0.0, above)
        below = jnp.where(sub < 4, pltpu.roll(fwd, 4, 0), pltpu.roll(fwd, 3, 0))
        below = jnp.where(sub == 7, 0.0, below)
        up = jnp.where(second, fwd, above)
        down = jnp.where(second, below, back)
        straight.append(31.0 * (up + down))
        to_right.append(31.0 * c + up)
        to_left.append(31.0 * c + down)
    zero = jnp.zeros((8, 128), jnp.float32)
    far_right = [pltpu.roll(v, 95, 1) for v in to_right] + [zero]
    far_left = [zero] + [pltpu.roll(v, 33, 1) for v in to_left]
    total = []
    for i in range(16):
        right = jnp.where(z_hi_half, far_right[i + 1], far_right[i])
        right = jnp.where(edge_hi, right, pltpu.roll(to_right[i], 127, 1))
        left = jnp.where(z_hi_half, far_left[i + 1], far_left[i])
        left = jnp.where(edge_lo, left, pltpu.roll(to_left[i], 1, 1))
        total.append(straight[i] + right + left)
    return total


def column(tile):
    return pl.ds(pl.multiple_of(tile * 128, 128), 128)


def times_factor(factor, row_of):
    def step(xy, totals):
        totals = list(totals)
        for s in range(8):
            row = row_of(xy, s)
            where = column((s % 4) * 32 + (s // 4) * 16 + xy)
            for i in range(8):
                totals[i] = totals[i] + factor[pl.ds(8 * i, 8), where] * row
        return tuple(totals)

    zero = jnp.zeros((8, 128), jnp.float32)
    totals = lax.fori_loop(0, 16, step, (zero,) * 8)
    return [jnp.sum(v, axis=1, keepdims=True) for v in totals]


def kernel(
    right_ref, diag_ref, factor_ref, out_ref,
    cells, factor, smooth, scale_ref, result,
    row_ref, row_in, chunk_ref, chunk_in, term, term_in, part, part_in,
    fix, fix_in, rhs_ref, term_b, term_b_in, last, last_in,
    load_sem, halo_send, halo_recv, send_sem, recv_sem,
):
    g, t = lax.axis_index("grp"), lax.axis_index("tile")
    z_hi, core, xy, z_lo = g // 2, g % 2, t // 2, t % 2
    m, z = core * 16 + xy, z_hi * 2 + z_lo
    rows_in, cols_in = pl.ds(HR, RD), pl.ds(HC, CD)

    loads = [
        pltpu.make_async_copy(right_ref, cells.at[0, rows_in, cols_in], load_sem.at[0]),
        pltpu.make_async_copy(diag_ref, cells.at[1, rows_in, cols_in], load_sem.at[1]),
        pltpu.make_async_copy(factor_ref, factor, load_sem.at[2]),
    ]
    for load in loads:
        load.start()

    barrier = pltpu.get_barrier_semaphore()

    def greet_z(k, _):
        pl.semaphore_signal(
            barrier, 1, device_id=device_at(m, (z + 1 + k) % N_Z), device_id_type=MESH
        )
        return _

    def greet_m(k, _):
        pl.semaphore_signal(
            barrier, 1, device_id=device_at((m + 1 + k) % N_LANE, z), device_id_type=MESH
        )
        return _

    lax.fori_loop(0, N_Z - 1, greet_z, 0)
    lax.fori_loop(0, N_LANE - 1, greet_m, 0)
    for a, b in DIRECTIONS:
        pl.semaphore_signal(
            barrier, 1,
            device_id=((g + a + N_GRP) % N_GRP, (t + b + N_TILE) % N_TILE),
            device_id_type=MESH,
        )

    def to_z(stage, source_of, target):
        def send(k, _):
            there = (z + 1 + k) % N_Z
            pltpu.make_async_remote_copy(
                src_ref=source_of(there), dst_ref=target.at[z],
                send_sem=send_sem.at[stage], recv_sem=recv_sem.at[stage],
                device_id=device_at(m, there), device_id_type=MESH,
            ).start()
            return _

        lax.fori_loop(0, N_Z - 1, send, 0)

    def send_m(stage, source, target, there):
        pltpu.make_async_remote_copy(
            src_ref=source, dst_ref=target.at[m],
            send_sem=send_sem.at[stage], recv_sem=recv_sem.at[stage],
            device_id=device_at(there, z), device_id_type=MESH,
        ).start()

    def to_m(stage, source, target):
        def send(k, _):
            send_m(stage, source, target, (m + 1 + k) % N_LANE)
            return _

        lax.fori_loop(0, N_LANE - 1, send, 0)

    def arrived(stage, target, count):
        blocks = target.at[pl.ds(0, count)]
        pltpu.make_async_copy(blocks, blocks, recv_sem.at[stage]).wait()

    def departed(stage, target, count):
        blocks = target.at[pl.ds(0, count)]
        pltpu.make_async_copy(blocks, blocks, send_sem.at[stage]).wait()

    loads[0].wait()
    row = restricted(cells[0, HR:HR + RD, HC:HC + CD], z_lo)
    row_ref[...] = row
    row_in[z] = row

    pl.semaphore_wait(barrier, N_Z - 1 + N_LANE - 1 + len(DIRECTIONS))
    to_z(0, lambda there: row_ref, row_in)

    loads[1].wait()
    row_from = {-1: HR, 0: HR, 1: RD}
    row_to = {-1: HR + RD, 0: HR, 1: 0}
    row_len = {-1: HR, 0: RD, 1: HR}
    col_from = {-1: HC, 0: HC, 1: CD}
    col_to = {-1: HC + CD, 0: HC, 1: 0}
    col_len = {-1: HC, 0: CD, 1: HC}
    halos = []
    for n, (a, b) in enumerate(DIRECTIONS):
        halos.append(pltpu.make_async_remote_copy(
            src_ref=cells.at[:, pl.ds(row_from[a], row_len[a]), pl.ds(col_from[b], col_len[b])],
            dst_ref=cells.at[:, pl.ds(row_to[a], row_len[a]), pl.ds(col_to[b], col_len[b])],
            send_sem=halo_send.at[n], recv_sem=halo_recv.at[n],
            device_id=((g + a + N_GRP) % N_GRP, (t + b + N_TILE) % N_TILE),
            device_id_type=MESH,
        ))
        halos[-1].start()

    arrived(0, row_in, N_Z - 1)
    chunk = jnp.concatenate([row_in[2 * i] + row_in[2 * i + 1] for i in range(4)], axis=0)
    chunk_ref[...] = chunk
    chunk_in[m] = chunk
    to_m(1, chunk_ref, chunk_in)

    for halo in halos:
        halo.wait_recv()
    line = g * RD - HR + lax.broadcasted_iota(jnp.int32, (ER, EC), 0)
    place = t * CD - HC + lanes((ER, EC))
    inside = (line >= 0) & (line < N_GRP * RD) & (place >= 0) & (place < N_TILE * CD)
    right_side = cells[0]
    diagonal = cells[1]
    scale = jnp.where(inside, 0.8 / (6.0 + diagonal), 0.0)
    scale_ref[...] = scale
    smoothed = scale * right_side
    for _ in range(3):
        smoothed = 0.2 * smoothed + scale * (right_side + beside(smoothed))
    smooth[...] = smoothed
    left_over = right_side - (6.0 + diagonal) * smoothed + beside(smoothed)
    part[4:5] = restricted(left_over[HR:HR + RD, HC:HC + CD], z_lo)
    part[5:6] = restricted(diagonal[HR:HR + RD, HC:HC + CD], z_lo)
    part[6:8] = jnp.zeros((2, 128), jnp.float32)

    def transposed(inner, stage, source, target):
        inner = [jnp.broadcast_to(v, (8, 128)) for v in inner]

        def term_of(there):
            for h in range(4):
                where = column(h * 32 + there)
                total = factor[pl.ds(0, 8), where] * inner[0]
                for i in range(1, 8):
                    total = total + factor[pl.ds(8 * i, 8), where] * inner[i]
                source[there, h:h + 1] = jnp.sum(total, axis=0, keepdims=True)

        def step(k, _):
            there = (m + 1 + k) % N_LANE
            term_of(there)
            send_m(stage, source.at[there], target, there)
            return _

        lax.fori_loop(0, N_LANE - 1, step, 0)
        term_of(m)
        target[m] = source[m]

    loads[2].wait()
    arrived(1, chunk_in, N_LANE - 1)
    inner = times_factor(factor, lambda i, s: chunk_in[(s // 4) * 16 + i, s % 4:s % 4 + 1])
    transposed(inner, 2, term, term_in)

    arrived(2, term_in, N_LANE - 1)
    part[0:4] = jnp.sum(term_in[...], axis=0)
    part_in[z] = part[...]
    to_z(3, lambda there: part, part_in)

    arrived(3, part_in, N_Z - 1)
    parts = [part_in[i] for i in range(N_Z)]
    coarse = functools.reduce(jnp.add, [v[0:4] for v in parts])
    rest = jnp.concatenate([parts[2 * i][4:5] + parts[2 * i + 1][4:5] for i in range(4)], axis=0)
    mean_diag = jnp.concatenate(
        [parts[2 * i][5:6] + parts[2 * i + 1][5:6] for i in range(4)], axis=0
    )
    own = rest - 0.5 * (126.0 / 256.0 + mean_diag) * coarse
    fix[...] = jnp.where(
        core == 0,
        jnp.concatenate([coarse, own], axis=0),
        jnp.concatenate([own, coarse], axis=0),
    )
    fix_in[m] = fix[...]
    to_m(4, fix, fix_in)

    arrived(4, fix_in, N_LANE - 1)
    low_rows = lax.broadcasted_iota(jnp.int32, (8, 128), 0) < 4
    field = [jnp.where(low_rows, fix_in[i], fix_in[16 + i]) for i in range(16)]
    around = coarse_neighbours(field)
    for i in range(16):
        own_i = pltpu.roll(jnp.where(low_rows, fix_in[16 + i], fix_in[i]), 4, 0)
        rhs_ref[i] = own_i + (0.5 / 256.0) * around[i]
    inner = times_factor(factor, lambda i, s: rhs_ref[i, s:s + 1])
    transposed(inner, 5, term_b, term_b_in)

    def coarse_rows(b):
        tt = t + b
        ok_t = (tt >= 0) & (tt < N_TILE)
        tt = (tt + N_TILE) % N_TILE
        rows = []
        for a, i_hi in ((-1, 1), (0, 0), (0, 1), (1, 0)):
            gg = g + a
            ok = ok_t & (gg >= 0) & (gg < N_GRP)
            gg = (gg + N_GRP) % N_GRP
            row = fix_in[(gg % 2) * 16 + tt // 2, pl.ds((gg % 2) * 4 + gg // 2, 1)]
            rows.append(quarter(row, tt % 2, i_hi, ok))
        return jnp.concatenate(rows + [jnp.zeros((4, 128), jnp.float32)], axis=0)

    lane8 = lanes((8, 128))
    at_left = jnp.sum(jnp.where(lane8 % 32 == 31, coarse_rows(-1), 0.0), axis=1, keepdims=True)
    at_right = jnp.sum(jnp.where(lane8 % 32 == 0, coarse_rows(1), 0.0), axis=1, keepdims=True)
    wide = 0.5 * jnp.concatenate(
        [
            jnp.broadcast_to(at_left, (8, HC)),
            spread_columns(coarse_rows(0)),
            jnp.broadcast_to(at_right, (8, HC)),
        ],
        axis=1,
    )
    fine = jnp.concatenate(
        [
            jnp.broadcast_to(wide[0:1], (HR, EC)),
            jnp.broadcast_to(wide[1:2], (FAC, EC)),
            jnp.broadcast_to(wide[2:3], (FAC, EC)),
            jnp.broadcast_to(wide[3:4], (HR, EC)),
        ],
        axis=0,
    )
    iterate = smooth[...] + fine
    residual = cells[0] - (6.0 + cells[1]) * iterate + beside(iterate)
    scale = scale_ref[...]
    smoothed = scale * residual
    for _ in range(3):
        smoothed = 0.2 * smoothed + scale * (residual + beside(smoothed))
    result[...] = (iterate + smoothed)[HR:HR + RD, HC:HC + CD]

    arrived(5, term_b_in, N_LANE - 1)
    summed = jnp.sum(term_b_in[...], axis=0)
    for i in range(4):
        last[i] = summed[i:i + 1]
    last_in[z] = last[z_hi]
    to_z(6, lambda there: last.at[there // 2], last_in)
    arrived(6, last_in, N_Z - 1)
    row = functools.reduce(jnp.add, [last_in[i] for i in range(N_Z)])
    pair = jnp.concatenate(
        [quarter(row, z_lo, 0, True), quarter(row, z_lo, 1, True), jnp.zeros((6, 128), jnp.float32)],
        axis=0,
    )
    pair = 0.5 * spread_columns(pair)
    out_ref[:FAC] = result[:FAC] + pair[0:1]
    out_ref[FAC:] = result[FAC:] + pair[1:2]

    for halo in halos:
        halo.wait_send()
    departed(0, row_in, N_Z - 1)
    departed(1, chunk_in, N_LANE - 1)
    departed(2, term_in, N_LANE - 1)
    departed(3, part_in, N_Z - 1)
    departed(4, fix_in, N_LANE - 1)
    departed(5, term_b_in, N_LANE - 1)
    departed(6, last_in, N_Z - 1)


def shards(right_side, diagonal, inverse_factor):
    f32 = jnp.float32
    return pl.pallas_call(
        kernel,
        out_shape=jax.ShapeDtypeStruct((RD, CD), f32),
        in_specs=[pl.BlockSpec(memory_space=pl.ANY)] * 3,
        out_specs=pl.BlockSpec(memory_space=pltpu.VMEM),
        scratch_shapes=[
            pltpu.VMEM((2, ER, EC), f32),
            pltpu.VMEM((CO, N_GRP * N_TILE * CO), f32),
            pltpu.VMEM((ER, EC), f32),
            pltpu.VMEM((ER, EC), f32),
            pltpu.VMEM((RD, CD), f32),
            pltpu.VMEM((1, 128), f32),
            pltpu.VMEM((N_Z, 1, 128), f32),
            pltpu.VMEM((4, 128), f32),
            pltpu.VMEM((N_LANE, 4, 128), f32),
            pltpu.VMEM((N_LANE, 4, 128), f32),
            pltpu.VMEM((N_LANE, 4, 128), f32),
            pltpu.VMEM((8, 128), f32),
            pltpu.VMEM((N_Z, 8, 128), f32),
            pltpu.VMEM((8, 128), f32),
            pltpu.VMEM((N_LANE, 8, 128), f32),
            pltpu.VMEM((16, 8, 128), f32),
            pltpu.VMEM((N_LANE, 4, 128), f32),
            pltpu.VMEM((N_LANE, 4, 128), f32),
            pltpu.VMEM((4, 1, 128), f32),
            pltpu.VMEM((N_Z, 1, 128), f32),
            pltpu.SemaphoreType.DMA((3,)),
            pltpu.SemaphoreType.DMA((len(DIRECTIONS),)),
            pltpu.SemaphoreType.DMA((len(DIRECTIONS),)),
            pltpu.SemaphoreType.DMA((7,)),
            pltpu.SemaphoreType.DMA((7,)),
        ],
        compiler_params=pltpu.CompilerParams(
            collective_id=0, has_side_effects=True, vmem_limit_bytes=24 * 1024 * 1024
        ),
    )(right_side, diagonal, inverse_factor)


def solution(mesh):
    placed = (P("grp", "tile"), P("grp", "tile"), P(("grp", "tile"), None))
    return jax.shard_map(
        shards, mesh=mesh, in_specs=placed, out_specs=P("grp", "tile"), check_vma=False
    )
```

```python
import functools

import jax
import jax.numpy as jnp
from jax import lax
from jax.experimental import pallas as pl
from jax.experimental.pallas import tpu as pltpu
from jax.sharding import PartitionSpec as P

MESH = pl.DeviceIdType.MESH
HIGHEST = lax.Precision.HIGHEST
RD, CD, FAC = 32, 512, 16
N_GRP, N_TILE = 8, 32
HR, HC = 8, 128
ER, EC = RD + 2 * HR, CD + 2 * HC
CO = 64
N_LANE, N_Z = 32, 8
OFFSETS = sorted(
    ((a, b) for a in range(4) for b in range(4)),
    key=lambda o: -(min(o[0], 4 - o[0]) + min(o[1], 4 - o[1])),
)
Z_OFFSETS = (4, 3, 5, 2, 6, 1, 7)
HOPS = 5
DIRECTIONS = [(a, b) for a in (-1, 0, 1) for b in (-1, 0, 1) if (a, b) != (0, 0)]


def hops(offset):
    return min(offset[0], 4 - offset[0]) + min(offset[1], 4 - offset[1])


def pick(k, values):
    out = jnp.int32(values[-1])
    for i, value in enumerate(values[:-1]):
        out = jnp.where(k == i, jnp.int32(value), out)
    return out


def beside(field):
    right = pltpu.roll(field, EC - 1, 1)
    left = pltpu.roll(field, 1, 1)
    return right + left + pltpu.roll(field + right, 1, 0) + pltpu.roll(field + left, ER - 1, 0)


def lanes(shape):
    return lax.broadcasted_iota(jnp.int32, shape, len(shape) - 1)


def restricted(block, z_lo):
    top = jnp.sum(block[:FAC], axis=0, keepdims=True)
    low = jnp.sum(block[FAC:], axis=0, keepdims=True)
    sums = jnp.concatenate([top, low, jnp.zeros((6, CD), jnp.float32)], axis=0)
    cell = lax.broadcasted_iota(jnp.int32, (CD, 128), 0) // FAC
    gather = jnp.where(cell == lanes((CD, 128)) % 32, 1.0 / (FAC * FAC), 0.0).astype(jnp.float32)
    means = jnp.dot(sums, gather, precision=HIGHEST, preferred_element_type=jnp.float32)
    lane = lanes((1, 128))
    row = jnp.where((lane // 32) % 2 == 0, means[0:1], means[1:2])
    return jnp.where(lane // 64 == z_lo, row, 0.0)


def spread_columns(rows):
    cell = lax.broadcasted_iota(jnp.int32, (128, CD), 0) % 32
    spread = jnp.where(cell == lanes((128, CD)) // FAC, 1.0, 0.0).astype(jnp.float32)
    return jnp.dot(rows, spread, precision=HIGHEST, preferred_element_type=jnp.float32)


def quarter(row, z_lo, i_hi, valid):
    lane = lanes((1, 128))
    keep = (lane // 32 == z_lo * 2 + i_hi) & valid
    return jnp.where(keep, row, 0.0)


def coarse_neighbours(field):
    sub = lax.broadcasted_iota(jnp.int32, (8, 128), 0)
    lane = lanes((8, 128))
    second = (lane // 32) % 2 == 1
    edge_hi, edge_lo = lane % 32 == 31, lane % 32 == 0
    z_hi_half = lane // 64 == 1
    straight, to_right, to_left = [], [], []
    for c in field:
        fwd = pltpu.roll(c, 32, 1)
        back = pltpu.roll(c, 96, 1)
        above = jnp.where(sub >= 4, pltpu.roll(back, 4, 0), pltpu.roll(back, 5, 0))
        above = jnp.where(sub == 0, 0.0, above)
        below = jnp.where(sub < 4, pltpu.roll(fwd, 4, 0), pltpu.roll(fwd, 3, 0))
        below = jnp.where(sub == 7, 0.0, below)
        up = jnp.where(second, fwd, above)
        down = jnp.where(second, below, back)
        straight.append(31.0 * (up + down))
        to_right.append(31.0 * c + up)
        to_left.append(31.0 * c + down)
    zero = jnp.zeros((8, 128), jnp.float32)
    far_right = [pltpu.roll(v, 95, 1) for v in to_right] + [zero]
    far_left = [zero] + [pltpu.roll(v, 33, 1) for v in to_left]
    total = []
    for i in range(16):
        right = jnp.where(z_hi_half, far_right[i + 1], far_right[i])
        right = jnp.where(edge_hi, right, pltpu.roll(to_right[i], 127, 1))
        left = jnp.where(z_hi_half, far_left[i + 1], far_left[i])
        left = jnp.where(edge_lo, left, pltpu.roll(to_left[i], 1, 1))
        total.append(straight[i] + right + left)
    return total


def column(tile):
    return pl.ds(pl.multiple_of(tile * 128, 128), 128)


def add_products(factor, totals, count, place_of, row_of):
    def step(k, totals):
        xy = place_of(k)
        totals = list(totals)
        for s in range(8):
            row = row_of(xy, s)
            where = column((s % 4) * 32 + (s // 4) * 16 + xy)
            for i in range(8):
                totals[i] = totals[i] + factor[pl.ds(8 * i, 8), where] * row
        return tuple(totals)

    if count == 1:
        return step(0, totals)
    return lax.fori_loop(0, count, step, totals)


def kernel(
    right_ref, diag_ref, factor_ref, out_ref,
    cells, factor, smooth, scale_ref, result,
    row_ref, row_in, chunk_ref, chunk_in, term, term_in, part, part_in,
    fix, fix_in, rhs_ref, term_b, term_b_in, last, last_in,
    load_sem, halo_send, halo_recv, send_sem, recv_sem, chunk_sem, fix_sem,
):
    g, t = lax.axis_index("grp"), lax.axis_index("tile")
    z_hi, core = lax.div(g, 2), lax.rem(g, 2)
    xy, z_lo = lax.div(t, 2), lax.rem(t, 2)
    x, y = lax.div(xy, 4), lax.rem(xy, 4)
    m, z = core * 16 + xy, z_hi * 2 + z_lo
    rows_in, cols_in = pl.ds(HR, RD), pl.ds(HC, CD)
    xs = [lax.rem(x + a, 4) for a in range(4)]
    ys = [lax.rem(y + b, 4) for b in range(4)]
    zs = [lax.rem(z + c, 8) for c in range(8)]
    mates = [
        (hops(o), (z_hi * 2 + c, xs[o[0]] * 8 + ys[o[1]] * 2 + z_lo))
        for o in OFFSETS[:-1] for c in range(2)
    ]
    mates.append((0, (z_hi * 2 + 1 - core, t)))
    column_mates = [
        (zs[c], (lax.div(zs[c], 2) * 2 + core, xy * 2 + lax.rem(zs[c], 2))) for c in Z_OFFSETS
    ]
    beside_here = [
        (lax.rem(g + a + N_GRP, N_GRP), lax.rem(t + b + N_TILE, N_TILE)) for a, b in DIRECTIONS
    ]

    barrier = pltpu.get_barrier_semaphore()
    for device in [d for _, d in column_mates] + [d for _, d in mates] + beside_here:
        pl.semaphore_signal(barrier, 1, device_id=device, device_id_type=MESH)

    loads = [
        pltpu.make_async_copy(right_ref, cells.at[0, rows_in, cols_in], load_sem.at[0]),
        pltpu.make_async_copy(diag_ref, cells.at[1, rows_in, cols_in], load_sem.at[1]),
        pltpu.make_async_copy(factor_ref, factor, load_sem.at[2]),
    ]
    for load in loads:
        load.start()

    def to_z(stage, source_of, target):
        for there, device in column_mates:
            pltpu.make_async_remote_copy(
                src_ref=source_of(there), dst_ref=target.at[z],
                send_sem=send_sem.at[stage], recv_sem=recv_sem.at[stage],
                device_id=device, device_id_type=MESH,
            ).start()

    def to_m(stage, source, target, near):
        for distance, device in mates:
            pltpu.make_async_remote_copy(
                src_ref=source, dst_ref=target.at[m],
                send_sem=send_sem.at[stage], recv_sem=near.at[distance],
                device_id=device, device_id_type=MESH,
            ).start()

    def arrived(sem, target, count):
        blocks = target.at[pl.ds(0, count)]
        pltpu.make_async_copy(blocks, blocks, sem).wait()

    def arrived_from(near, target, distance):
        arrived(near.at[distance], target, sum(d == distance for d, _ in mates))

    def departed(stage, target, count):
        blocks = target.at[pl.ds(0, count)]
        pltpu.make_async_copy(blocks, blocks, send_sem.at[stage]).wait()

    loads[0].wait()
    row = restricted(cells[0, HR:HR + RD, HC:HC + CD], z_lo)
    row_ref[...] = row
    row_in[z] = row

    pl.semaphore_wait(barrier, N_Z - 1 + N_LANE - 1 + len(DIRECTIONS))
    to_z(0, lambda there: row_ref, row_in)

    loads[1].wait()
    row_from = {-1: HR, 0: HR, 1: RD}
    row_to = {-1: HR + RD, 0: HR, 1: 0}
    row_len = {-1: HR, 0: RD, 1: HR}
    col_from = {-1: HC, 0: HC, 1: CD}
    col_to = {-1: HC + CD, 0: HC, 1: 0}
    col_len = {-1: HC, 0: CD, 1: HC}
    halos = []
    for n, (a, b) in enumerate(DIRECTIONS):
        halos.append(pltpu.make_async_remote_copy(
            src_ref=cells.at[:, pl.ds(row_from[a], row_len[a]), pl.ds(col_from[b], col_len[b])],
            dst_ref=cells.at[:, pl.ds(row_to[a], row_len[a]), pl.ds(col_to[b], col_len[b])],
            send_sem=halo_send.at[n], recv_sem=halo_recv.at[n],
            device_id=beside_here[n],
            device_id_type=MESH,
        ))
        halos[-1].start()

    arrived(recv_sem.at[0], row_in, N_Z - 1)
    chunk = jnp.concatenate([row_in[2 * i] + row_in[2 * i + 1] for i in range(4)], axis=0)
    chunk_ref[...] = chunk
    chunk_in[m] = chunk
    to_m(1, chunk_ref, chunk_in, chunk_sem)

    for halo in halos:
        halo.wait_recv()
    line = g * RD - HR + lax.broadcasted_iota(jnp.int32, (ER, EC), 0)
    place = t * CD - HC + lanes((ER, EC))
    inside = (line >= 0) & (line < N_GRP * RD) & (place >= 0) & (place < N_TILE * CD)
    right_side = cells[0]
    diagonal = cells[1]
    scale = jnp.where(inside, 0.8 / (6.0 + diagonal), 0.0)
    scale_ref[...] = scale
    smoothed = scale * right_side
    for _ in range(3):
        smoothed = 0.2 * smoothed + scale * (right_side + beside(smoothed))
    smooth[...] = smoothed
    left_over = right_side - (6.0 + diagonal) * smoothed + beside(smoothed)
    part[4:5] = restricted(left_over[HR:HR + RD, HC:HC + CD], z_lo)
    part[5:6] = restricted(diagonal[HR:HR + RD, HC:HC + CD], z_lo)
    part[6:8] = jnp.zeros((2, 128), jnp.float32)

    def transposed(inner, stage, source, target):
        inner = [jnp.broadcast_to(v, (8, 128)) for v in inner]

        def term_of(there):
            for h in range(4):
                where = column(h * 32 + there)
                total = factor[pl.ds(0, 8), where] * inner[0]
                for i in range(1, 8):
                    total = total + factor[pl.ds(8 * i, 8), where] * inner[i]
                source[there, h:h + 1] = jnp.sum(total, axis=0, keepdims=True)

        def send(there, device):
            pltpu.make_async_remote_copy(
                src_ref=source.at[there], dst_ref=target.at[m],
                send_sem=send_sem.at[stage], recv_sem=recv_sem.at[stage],
                device_id=device, device_id_type=MESH,
            ).start()

        def step(k, _):
            xx = lax.rem(x + pick(k, [o[0] for o in OFFSETS]), 4)
            yy = lax.rem(y + pick(k, [o[1] for o in OFFSETS]), 4)
            for c in range(2):
                there = c * 16 + xx * 4 + yy
                term_of(there)
                send(there, (z_hi * 2 + c, xx * 8 + yy * 2 + z_lo))
            return _

        lax.fori_loop(0, len(OFFSETS) - 1, step, 0)
        other = (1 - core) * 16 + xy
        term_of(other)
        send(other, (z_hi * 2 + 1 - core, t))
        term_of(m)
        target[m] = source[m]

    none = (jnp.zeros((8, 128), jnp.float32),) * 8

    def summed_lanes(totals):
        return [jnp.sum(v, axis=1, keepdims=True) for v in totals]

    loads[2].wait()
    totals = none
    for group in ((0, 1, 2), (3,), (4,)):
        for distance in group:
            arrived_from(chunk_sem, chunk_in, distance)
        members = [o for o in OFFSETS if hops(o) in group]
        totals = add_products(
            factor, totals, len(members),
            lambda k: (lax.rem(x + pick(k, [o[0] for o in members]), 4) * 4
                       + lax.rem(y + pick(k, [o[1] for o in members]), 4)),
            lambda i, s: chunk_in[(s // 4) * 16 + i, s % 4:s % 4 + 1],
        )
    transposed(summed_lanes(totals), 2, term, term_in)

    arrived(recv_sem.at[2], term_in, N_LANE - 1)
    part[0:4] = jnp.sum(term_in[...], axis=0)
    part_in[z] = part[...]
    to_z(3, lambda there: part, part_in)

    arrived(recv_sem.at[3], part_in, N_Z - 1)
    parts = [part_in[i] for i in range(N_Z)]
    coarse = functools.reduce(jnp.add, [v[0:4] for v in parts])
    rest = jnp.concatenate([parts[2 * i][4:5] + parts[2 * i + 1][4:5] for i in range(4)], axis=0)
    mean_diag = jnp.concatenate(
        [parts[2 * i][5:6] + parts[2 * i + 1][5:6] for i in range(4)], axis=0
    )
    own = rest - 0.5 * (126.0 / 256.0 + mean_diag) * coarse
    fix[...] = jnp.where(
        core == 0,
        jnp.concatenate([coarse, own], axis=0),
        jnp.concatenate([own, coarse], axis=0),
    )
    fix_in[m] = fix[...]
    to_m(4, fix, fix_in, fix_sem)

    for distance in range(HOPS):
        arrived_from(fix_sem, fix_in, distance)
    low_rows = lax.broadcasted_iota(jnp.int32, (8, 128), 0) < 4
    field = [jnp.where(low_rows, fix_in[i], fix_in[16 + i]) for i in range(16)]
    around = coarse_neighbours(field)
    for i in range(16):
        own_i = pltpu.roll(jnp.where(low_rows, fix_in[16 + i], fix_in[i]), 4, 0)
        rhs_ref[i] = own_i + (0.5 / 256.0) * around[i]
    totals = add_products(factor, none, 16, lambda k: k, lambda i, s: rhs_ref[i, s:s + 1])
    transposed(summed_lanes(totals), 5, term_b, term_b_in)

    def coarse_rows(b):
        tt = t + b
        ok_t = (tt >= 0) & (tt < N_TILE)
        tt = (tt + N_TILE) % N_TILE
        rows = []
        for a, i_hi in ((-1, 1), (0, 0), (0, 1), (1, 0)):
            gg = g + a
            ok = ok_t & (gg >= 0) & (gg < N_GRP)
            gg = (gg + N_GRP) % N_GRP
            row = fix_in[(gg % 2) * 16 + tt // 2, pl.ds((gg % 2) * 4 + gg // 2, 1)]
            rows.append(quarter(row, tt % 2, i_hi, ok))
        return jnp.concatenate(rows + [jnp.zeros((4, 128), jnp.float32)], axis=0)

    lane8 = lanes((8, 128))
    at_left = jnp.sum(jnp.where(lane8 % 32 == 31, coarse_rows(-1), 0.0), axis=1, keepdims=True)
    at_right = jnp.sum(jnp.where(lane8 % 32 == 0, coarse_rows(1), 0.0), axis=1, keepdims=True)
    wide = 0.5 * jnp.concatenate(
        [
            jnp.broadcast_to(at_left, (8, HC)),
            spread_columns(coarse_rows(0)),
            jnp.broadcast_to(at_right, (8, HC)),
        ],
        axis=1,
    )
    fine = jnp.concatenate(
        [
            jnp.broadcast_to(wide[0:1], (HR, EC)),
            jnp.broadcast_to(wide[1:2], (FAC, EC)),
            jnp.broadcast_to(wide[2:3], (FAC, EC)),
            jnp.broadcast_to(wide[3:4], (HR, EC)),
        ],
        axis=0,
    )
    iterate = smooth[...] + fine
    residual = cells[0] - (6.0 + cells[1]) * iterate + beside(iterate)
    scale = scale_ref[...]
    smoothed = scale * residual
    for _ in range(3):
        smoothed = 0.2 * smoothed + scale * (residual + beside(smoothed))
    result[...] = (iterate + smoothed)[HR:HR + RD, HC:HC + CD]

    arrived(recv_sem.at[5], term_b_in, N_LANE - 1)
    summed = jnp.sum(term_b_in[...], axis=0)
    for i in range(4):
        last[i] = summed[i:i + 1]
    last_in[z] = last[z_hi]
    to_z(6, lambda there: last.at[lax.div(there, 2)], last_in)
    arrived(recv_sem.at[6], last_in, N_Z - 1)
    row = functools.reduce(jnp.add, [last_in[i] for i in range(N_Z)])
    pair = jnp.concatenate(
        [quarter(row, z_lo, 0, True), quarter(row, z_lo, 1, True), jnp.zeros((6, 128), jnp.float32)],
        axis=0,
    )
    pair = 0.5 * spread_columns(pair)
    out_ref[:FAC] = result[:FAC] + pair[0:1]
    out_ref[FAC:] = result[FAC:] + pair[1:2]

    for halo in halos:
        halo.wait_send()
    departed(0, row_in, N_Z - 1)
    departed(1, chunk_in, N_LANE - 1)
    departed(2, term_in, N_LANE - 1)
    departed(3, part_in, N_Z - 1)
    departed(4, fix_in, N_LANE - 1)
    departed(5, term_b_in, N_LANE - 1)
    departed(6, last_in, N_Z - 1)


def shards(right_side, diagonal, inverse_factor):
    f32 = jnp.float32
    return pl.pallas_call(
        kernel,
        out_shape=jax.ShapeDtypeStruct((RD, CD), f32),
        in_specs=[pl.BlockSpec(memory_space=pltpu.HBM)] * 3,
        out_specs=pl.BlockSpec(memory_space=pltpu.VMEM),
        scratch_shapes=[
            pltpu.VMEM((2, ER, EC), f32),
            pltpu.VMEM((CO, N_GRP * N_TILE * CO), f32),
            pltpu.VMEM((ER, EC), f32),
            pltpu.VMEM((ER, EC), f32),
            pltpu.VMEM((RD, CD), f32),
            pltpu.VMEM((1, 128), f32),
            pltpu.VMEM((N_Z, 1, 128), f32),
            pltpu.VMEM((4, 128), f32),
            pltpu.VMEM((N_LANE, 4, 128), f32),
            pltpu.VMEM((N_LANE, 4, 128), f32),
            pltpu.VMEM((N_LANE, 4, 128), f32),
            pltpu.VMEM((8, 128), f32),
            pltpu.VMEM((N_Z, 8, 128), f32),
            pltpu.VMEM((8, 128), f32),
            pltpu.VMEM((N_LANE, 8, 128), f32),
            pltpu.VMEM((16, 8, 128), f32),
            pltpu.VMEM((N_LANE, 4, 128), f32),
            pltpu.VMEM((N_LANE, 4, 128), f32),
            pltpu.VMEM((4, 1, 128), f32),
            pltpu.VMEM((N_Z, 1, 128), f32),
            pltpu.SemaphoreType.DMA((3,)),
            pltpu.SemaphoreType.DMA((len(DIRECTIONS),)),
            pltpu.SemaphoreType.DMA((len(DIRECTIONS),)),
            pltpu.SemaphoreType.DMA((7,)),
            pltpu.SemaphoreType.DMA((7,)),
            pltpu.SemaphoreType.DMA((HOPS,)),
            pltpu.SemaphoreType.DMA((HOPS,)),
        ],
        compiler_params=pltpu.CompilerParams(
            collective_id=0, has_side_effects=True, vmem_limit_bytes=60 * 1024 * 1024
        ),
    )(right_side, diagonal, inverse_factor)


def solution(mesh):
    placed = (P("grp", "tile"), P("grp", "tile"), P(("grp", "tile"), None))
    return jax.shard_map(
        shards, mesh=mesh, in_specs=placed, out_specs=P("grp", "tile"), check_vma=False
    )
```

```python
import functools

import jax
import jax.numpy as jnp
from jax import lax
from jax.experimental import pallas as pl
from jax.experimental.pallas import tpu as pltpu
from jax.sharding import PartitionSpec as P

MESH = pl.DeviceIdType.MESH
HIGHEST = lax.Precision.HIGHEST
RD, CD, FAC = 32, 512, 16
N_GRP, N_TILE = 8, 32
HR, HC = 8, 128
ER, EC = RD + 2 * HR, CD + 2 * HC
CO = 64
N_LANE, N_Z = 32, 8
OFFSETS = sorted(
    ((a, b) for a in range(4) for b in range(4)),
    key=lambda o: -(min(o[0], 4 - o[0]) + min(o[1], 4 - o[1])),
)
Z_OFFSETS = (4, 3, 5, 2, 6, 1, 7)
HOPS = 5
DIRECTIONS = [(a, b) for a in (-1, 0, 1) for b in (-1, 0, 1) if (a, b) != (0, 0)]


def hops(offset):
    return min(offset[0], 4 - offset[0]) + min(offset[1], 4 - offset[1])


def pick(k, values):
    out = jnp.int32(values[-1])
    for i, value in enumerate(values[:-1]):
        out = jnp.where(k == i, jnp.int32(value), out)
    return out


def beside(field):
    right = pltpu.roll(field, EC - 1, 1)
    left = pltpu.roll(field, 1, 1)
    return right + left + pltpu.roll(field + right, 1, 0) + pltpu.roll(field + left, ER - 1, 0)


def lanes(shape):
    return lax.broadcasted_iota(jnp.int32, shape, len(shape) - 1)


def restricted(block, z_lo):
    top = jnp.sum(block[:FAC], axis=0, keepdims=True)
    low = jnp.sum(block[FAC:], axis=0, keepdims=True)
    sums = jnp.concatenate([top, low, jnp.zeros((6, CD), jnp.float32)], axis=0)
    cell = lax.broadcasted_iota(jnp.int32, (CD, 128), 0) // FAC
    gather = jnp.where(cell == lanes((CD, 128)) % 32, 1.0 / (FAC * FAC), 0.0).astype(jnp.float32)
    means = jnp.dot(sums, gather, precision=HIGHEST, preferred_element_type=jnp.float32)
    lane = lanes((1, 128))
    row = jnp.where((lane // 32) % 2 == 0, means[0:1], means[1:2])
    return jnp.where(lane // 64 == z_lo, row, 0.0)


def spread_columns(rows):
    cell = lax.broadcasted_iota(jnp.int32, (128, CD), 0) % 32
    spread = jnp.where(cell == lanes((128, CD)) // FAC, 1.0, 0.0).astype(jnp.float32)
    return jnp.dot(rows, spread, precision=HIGHEST, preferred_element_type=jnp.float32)


def quarter(row, z_lo, i_hi, valid):
    lane = lanes((1, 128))
    keep = (lane // 32 == z_lo * 2 + i_hi) & valid
    return jnp.where(keep, row, 0.0)


def coarse_neighbours(field):
    sub = lax.broadcasted_iota(jnp.int32, (8, 128), 0)
    lane = lanes((8, 128))
    second = (lane // 32) % 2 == 1
    edge_hi, edge_lo = lane % 32 == 31, lane % 32 == 0
    z_hi_half = lane // 64 == 1
    straight, to_right, to_left = [], [], []
    for c in field:
        fwd = pltpu.roll(c, 32, 1)
        back = pltpu.roll(c, 96, 1)
        above = jnp.where(sub >= 4, pltpu.roll(back, 4, 0), pltpu.roll(back, 5, 0))
        above = jnp.where(sub == 0, 0.0, above)
        below = jnp.where(sub < 4, pltpu.roll(fwd, 4, 0), pltpu.roll(fwd, 3, 0))
        below = jnp.where(sub == 7, 0.0, below)
        up = jnp.where(second, fwd, above)
        down = jnp.where(second, below, back)
        straight.append(31.0 * (up + down))
        to_right.append(31.0 * c + up)
        to_left.append(31.0 * c + down)
    zero = jnp.zeros((8, 128), jnp.float32)
    far_right = [pltpu.roll(v, 95, 1) for v in to_right] + [zero]
    far_left = [zero] + [pltpu.roll(v, 33, 1) for v in to_left]
    total = []
    for i in range(16):
        right = jnp.where(z_hi_half, far_right[i + 1], far_right[i])
        right = jnp.where(edge_hi, right, pltpu.roll(to_right[i], 127, 1))
        left = jnp.where(z_hi_half, far_left[i + 1], far_left[i])
        left = jnp.where(edge_lo, left, pltpu.roll(to_left[i], 1, 1))
        total.append(straight[i] + right + left)
    return total


def column(tile):
    return pl.ds(pl.multiple_of(tile * 128, 128), 128)


def add_products(factor, totals, count, place_of, row_of):
    def step(k, totals):
        xy = place_of(k)
        totals = list(totals)
        for s in range(8):
            row = row_of(xy, s)
            where = column((s % 4) * 32 + (s // 4) * 16 + xy)
            for i in range(8):
                totals[i] = totals[i] + factor[pl.ds(8 * i, 8), where] * row
        return tuple(totals)

    if count == 1:
        return step(0, totals)
    return lax.fori_loop(0, count, step, totals)


def kernel(
    right_ref, diag_ref, factor_ref, out_ref,
    cells, factor, smooth, scale_ref, result,
    row_ref, row_in, chunk_ref, chunk_in, term, term_in, part, part_in,
    fix, fix_in, rhs_ref, last, last_in,
    load_sem, halo_send, halo_recv, send_sem, recv_sem, chunk_sem, fix_sem, last_sem,
):
    g, t = lax.axis_index("grp"), lax.axis_index("tile")
    z_hi, core = lax.div(g, 2), lax.rem(g, 2)
    xy, z_lo = lax.div(t, 2), lax.rem(t, 2)
    x, y = lax.div(xy, 4), lax.rem(xy, 4)
    m, z = core * 16 + xy, z_hi * 2 + z_lo
    rows_in, cols_in = pl.ds(HR, RD), pl.ds(HC, CD)
    xs = [lax.rem(x + a, 4) for a in range(4)]
    ys = [lax.rem(y + b, 4) for b in range(4)]
    zs = [lax.rem(z + c, 8) for c in range(8)]
    mates = [
        (hops(o), (z_hi * 2 + c, xs[o[0]] * 8 + ys[o[1]] * 2 + z_lo))
        for o in OFFSETS[:-1] for c in range(2)
    ]
    mates.append((0, (z_hi * 2 + 1 - core, t)))
    column_mates = [
        (zs[c], (lax.div(zs[c], 2) * 2 + core, xy * 2 + lax.rem(zs[c], 2))) for c in Z_OFFSETS
    ]
    beside_here = [
        (lax.rem(g + a + N_GRP, N_GRP), lax.rem(t + b + N_TILE, N_TILE)) for a, b in DIRECTIONS
    ]

    barrier = pltpu.get_barrier_semaphore()
    for device in [d for _, d in column_mates] + [d for _, d in mates] + beside_here:
        pl.semaphore_signal(barrier, 1, device_id=device, device_id_type=MESH)

    loads = [
        pltpu.make_async_copy(right_ref, cells.at[0, rows_in, cols_in], load_sem.at[0]),
        pltpu.make_async_copy(diag_ref, cells.at[1, rows_in, cols_in], load_sem.at[1]),
        pltpu.make_async_copy(factor_ref, factor, load_sem.at[2]),
    ]
    for load in loads:
        load.start()

    def to_z(stage, source_of, target):
        for there, device in column_mates:
            pltpu.make_async_remote_copy(
                src_ref=source_of(there), dst_ref=target.at[z],
                send_sem=send_sem.at[stage], recv_sem=recv_sem.at[stage],
                device_id=device, device_id_type=MESH,
            ).start()

    def to_m(stage, source, target, near):
        for distance, device in mates:
            pltpu.make_async_remote_copy(
                src_ref=source, dst_ref=target.at[m],
                send_sem=send_sem.at[stage], recv_sem=near.at[distance],
                device_id=device, device_id_type=MESH,
            ).start()

    def arrived(sem, target, count):
        blocks = target.at[pl.ds(0, count)]
        pltpu.make_async_copy(blocks, blocks, sem).wait()

    def arrived_from(near, target, distance):
        arrived(near.at[distance], target, sum(d == distance for d, _ in mates))

    def departed(stage, target, count):
        blocks = target.at[pl.ds(0, count)]
        pltpu.make_async_copy(blocks, blocks, send_sem.at[stage]).wait()

    loads[0].wait()
    row = restricted(cells[0, HR:HR + RD, HC:HC + CD], z_lo)
    row_ref[...] = row
    row_in[z] = row

    pl.semaphore_wait(barrier, N_Z - 1 + N_LANE - 1 + len(DIRECTIONS))
    to_z(0, lambda there: row_ref, row_in)

    loads[1].wait()
    row_from = {-1: HR, 0: HR, 1: RD}
    row_to = {-1: HR + RD, 0: HR, 1: 0}
    row_len = {-1: HR, 0: RD, 1: HR}
    col_from = {-1: HC, 0: HC, 1: CD}
    col_to = {-1: HC + CD, 0: HC, 1: 0}
    col_len = {-1: HC, 0: CD, 1: HC}
    halos = []
    for n, (a, b) in enumerate(DIRECTIONS):
        halos.append(pltpu.make_async_remote_copy(
            src_ref=cells.at[:, pl.ds(row_from[a], row_len[a]), pl.ds(col_from[b], col_len[b])],
            dst_ref=cells.at[:, pl.ds(row_to[a], row_len[a]), pl.ds(col_to[b], col_len[b])],
            send_sem=halo_send.at[n], recv_sem=halo_recv.at[n],
            device_id=beside_here[n],
            device_id_type=MESH,
        ))
        halos[-1].start()

    arrived(recv_sem.at[0], row_in, N_Z - 1)
    chunk = jnp.concatenate([row_in[2 * i] + row_in[2 * i + 1] for i in range(4)], axis=0)
    chunk_ref[...] = chunk
    chunk_in[m] = chunk
    to_m(1, chunk_ref, chunk_in, chunk_sem)

    for halo in halos:
        halo.wait_recv()
    line = g * RD - HR + lax.broadcasted_iota(jnp.int32, (ER, EC), 0)
    place = t * CD - HC + lanes((ER, EC))
    inside = (line >= 0) & (line < N_GRP * RD) & (place >= 0) & (place < N_TILE * CD)
    right_side = cells[0]
    diagonal = cells[1]
    scale = jnp.where(inside, 0.8 / (6.0 + diagonal), 0.0)
    scale_ref[...] = scale
    smoothed = scale * right_side
    for _ in range(3):
        smoothed = 0.2 * smoothed + scale * (right_side + beside(smoothed))
    smooth[...] = smoothed
    left_over = right_side - (6.0 + diagonal) * smoothed + beside(smoothed)
    part[4:5] = restricted(left_over[HR:HR + RD, HC:HC + CD], z_lo)
    part[5:6] = restricted(diagonal[HR:HR + RD, HC:HC + CD], z_lo)
    part[6:8] = jnp.zeros((2, 128), jnp.float32)

    def transposed(inner, store, send):
        inner = [jnp.broadcast_to(v, (8, 128)) for v in inner]

        def term_of(there):
            for h in range(4):
                where = column(h * 32 + there)
                total = factor[pl.ds(0, 8), where] * inner[0]
                for i in range(1, 8):
                    total = total + factor[pl.ds(8 * i, 8), where] * inner[i]
                store(there, h, jnp.sum(total, axis=0, keepdims=True))

        def step(k, _):
            xx = lax.rem(x + pick(k, [o[0] for o in OFFSETS]), 4)
            yy = lax.rem(y + pick(k, [o[1] for o in OFFSETS]), 4)
            for c in range(2):
                term_of(c * 16 + xx * 4 + yy)
                send(c, xx * 4 + yy, k)
            return _

        lax.fori_loop(0, len(OFFSETS) - 1, step, 0)
        term_of((1 - core) * 16 + xy)
        send(1 - core, xy, len(OFFSETS) - 1)
        term_of(m)

    def store_term(there, h, row):
        term[there, h:h + 1] = row

    def send_term(c, there, k):
        pltpu.make_async_remote_copy(
            src_ref=term.at[c * 16 + there], dst_ref=term_in.at[m],
            send_sem=send_sem.at[2], recv_sem=recv_sem.at[2],
            device_id=(z_hi * 2 + c, there * 2 + z_lo), device_id_type=MESH,
        ).start()

    def store_last(there, h, row):
        last[there, h] = row

    def send_last(c, there, k, places=(*Z_OFFSETS, 0)):
        distance = pick(k, [hops(o) for o in OFFSETS]) if k is not len(OFFSETS) - 1 else 0
        for i, o in enumerate(places):
            half = lax.div(zs[o], 2)
            pltpu.make_async_remote_copy(
                src_ref=last.at[c * 16 + there, half],
                dst_ref=last_in.at[(k * 2 + core) * N_Z + i],
                send_sem=send_sem.at[4], recv_sem=last_sem.at[distance],
                device_id=(half * 2 + c, there * 2 + lax.rem(zs[o], 2)), device_id_type=MESH,
            ).start()

    none = (jnp.zeros((8, 128), jnp.float32),) * 8

    def summed_lanes(totals):
        return [jnp.sum(v, axis=1, keepdims=True) for v in totals]

    loads[2].wait()
    totals = none
    for group in ((0, 1, 2), (3,), (4,)):
        for distance in group:
            arrived_from(chunk_sem, chunk_in, distance)
        members = [o for o in OFFSETS if hops(o) in group]
        totals = add_products(
            factor, totals, len(members),
            lambda k: (lax.rem(x + pick(k, [o[0] for o in members]), 4) * 4
                       + lax.rem(y + pick(k, [o[1] for o in members]), 4)),
            lambda i, s: chunk_in[(s // 4) * 16 + i, s % 4:s % 4 + 1],
        )
    transposed(summed_lanes(totals), store_term, send_term)
    term_in[m] = term[m]

    arrived(recv_sem.at[2], term_in, N_LANE - 1)
    part[0:4] = jnp.sum(term_in[...], axis=0)
    part_in[z] = part[...]
    to_z(3, lambda there: part, part_in)

    arrived(recv_sem.at[3], part_in, N_Z - 1)
    parts = [part_in[i] for i in range(N_Z)]
    coarse = functools.reduce(jnp.add, [v[0:4] for v in parts])
    rest = jnp.concatenate([parts[2 * i][4:5] + parts[2 * i + 1][4:5] for i in range(4)], axis=0)
    mean_diag = jnp.concatenate(
        [parts[2 * i][5:6] + parts[2 * i + 1][5:6] for i in range(4)], axis=0
    )
    own = rest - 0.5 * (126.0 / 256.0 + mean_diag) * coarse
    fix[...] = jnp.where(
        core == 0,
        jnp.concatenate([coarse, own], axis=0),
        jnp.concatenate([own, coarse], axis=0),
    )
    fix_in[m] = fix[...]
    to_m(5, fix, fix_in, fix_sem)

    for distance in range(HOPS):
        arrived_from(fix_sem, fix_in, distance)
    low_rows = lax.broadcasted_iota(jnp.int32, (8, 128), 0) < 4
    field = [jnp.where(low_rows, fix_in[i], fix_in[16 + i]) for i in range(16)]
    around = coarse_neighbours(field)
    for i in range(16):
        own_i = pltpu.roll(jnp.where(low_rows, fix_in[16 + i], fix_in[i]), 4, 0)
        rhs_ref[i] = own_i + (0.5 / 256.0) * around[i]
    totals = add_products(factor, none, 16, lambda k: k, lambda i, s: rhs_ref[i, s:s + 1])
    transposed(summed_lanes(totals), store_last, send_last)
    send_last(core, xy, len(OFFSETS) - 1, Z_OFFSETS)
    last_in[((len(OFFSETS) - 1) * 2 + core) * N_Z + N_Z - 1] = last[m, z_hi]

    def coarse_rows(b):
        tt = t + b
        ok_t = (tt >= 0) & (tt < N_TILE)
        tt = (tt + N_TILE) % N_TILE
        rows = []
        for a, i_hi in ((-1, 1), (0, 0), (0, 1), (1, 0)):
            gg = g + a
            ok = ok_t & (gg >= 0) & (gg < N_GRP)
            gg = (gg + N_GRP) % N_GRP
            row = fix_in[(gg % 2) * 16 + tt // 2, pl.ds((gg % 2) * 4 + gg // 2, 1)]
            rows.append(quarter(row, tt % 2, i_hi, ok))
        return jnp.concatenate(rows + [jnp.zeros((4, 128), jnp.float32)], axis=0)

    lane8 = lanes((8, 128))
    at_left = jnp.sum(jnp.where(lane8 % 32 == 31, coarse_rows(-1), 0.0), axis=1, keepdims=True)
    at_right = jnp.sum(jnp.where(lane8 % 32 == 0, coarse_rows(1), 0.0), axis=1, keepdims=True)
    wide = 0.5 * jnp.concatenate(
        [
            jnp.broadcast_to(at_left, (8, HC)),
            spread_columns(coarse_rows(0)),
            jnp.broadcast_to(at_right, (8, HC)),
        ],
        axis=1,
    )
    fine = jnp.concatenate(
        [
            jnp.broadcast_to(wide[0:1], (HR, EC)),
            jnp.broadcast_to(wide[1:2], (FAC, EC)),
            jnp.broadcast_to(wide[2:3], (FAC, EC)),
            jnp.broadcast_to(wide[3:4], (HR, EC)),
        ],
        axis=0,
    )
    iterate = smooth[...] + fine
    residual = cells[0] - (6.0 + cells[1]) * iterate + beside(iterate)
    scale = scale_ref[...]
    smoothed = scale * residual
    for _ in range(3):
        smoothed = 0.2 * smoothed + scale * (residual + beside(smoothed))
    result[...] = (iterate + smoothed)[HR:HR + RD, HC:HC + CD]

    row = jnp.zeros((1, 128), jnp.float32)
    for distance in range(HOPS):
        places = [k for k, o in enumerate(OFFSETS) if hops(o) == distance]
        first, count = places[0] * 2 * N_Z, len(places) * 2 * N_Z
        arrived(last_sem.at[distance], last_in, count - (distance == 0))
        row = row + jnp.sum(last_in[first:first + count], axis=0)
    pair = jnp.concatenate(
        [quarter(row, z_lo, 0, True), quarter(row, z_lo, 1, True), jnp.zeros((6, 128), jnp.float32)],
        axis=0,
    )
    pair = 0.5 * spread_columns(pair)
    out_ref[:FAC] = result[:FAC] + pair[0:1]
    out_ref[FAC:] = result[FAC:] + pair[1:2]

    for halo in halos:
        halo.wait_send()
    departed(0, row_in, N_Z - 1)
    departed(1, chunk_in, N_LANE - 1)
    departed(2, term_in, N_LANE - 1)
    departed(3, part_in, N_Z - 1)
    departed(5, fix_in, N_LANE - 1)
    departed(4, last_in, N_GRP * N_TILE - 1)


def shards(right_side, diagonal, inverse_factor):
    f32 = jnp.float32
    return pl.pallas_call(
        kernel,
        out_shape=jax.ShapeDtypeStruct((RD, CD), f32),
        in_specs=[pl.BlockSpec(memory_space=pltpu.HBM)] * 3,
        out_specs=pl.BlockSpec(memory_space=pltpu.VMEM),
        scratch_shapes=[
            pltpu.VMEM((2, ER, EC), f32),
            pltpu.VMEM((CO, N_GRP * N_TILE * CO), f32),
            pltpu.VMEM((ER, EC), f32),
            pltpu.VMEM((ER, EC), f32),
            pltpu.VMEM((RD, CD), f32),
            pltpu.VMEM((1, 128), f32),
            pltpu.VMEM((N_Z, 1, 128), f32),
            pltpu.VMEM((4, 128), f32),
            pltpu.VMEM((N_LANE, 4, 128), f32),
            pltpu.VMEM((N_LANE, 4, 128), f32),
            pltpu.VMEM((N_LANE, 4, 128), f32),
            pltpu.VMEM((8, 128), f32),
            pltpu.VMEM((N_Z, 8, 128), f32),
            pltpu.VMEM((8, 128), f32),
            pltpu.VMEM((N_LANE, 8, 128), f32),
            pltpu.VMEM((16, 8, 128), f32),
            pltpu.VMEM((N_LANE, 4, 1, 128), f32),
            pltpu.VMEM((N_GRP * N_TILE, 1, 128), f32),
            pltpu.SemaphoreType.DMA((3,)),
            pltpu.SemaphoreType.DMA((len(DIRECTIONS),)),
            pltpu.SemaphoreType.DMA((len(DIRECTIONS),)),
            pltpu.SemaphoreType.DMA((6,)),
            pltpu.SemaphoreType.DMA((4,)),
            pltpu.SemaphoreType.DMA((HOPS,)),
            pltpu.SemaphoreType.DMA((HOPS,)),
            pltpu.SemaphoreType.DMA((HOPS,)),
        ],
        compiler_params=pltpu.CompilerParams(
            collective_id=0, has_side_effects=True, vmem_limit_bytes=55160 * 1024
        ),
    )(right_side, diagonal, inverse_factor)


def solution(mesh):
    placed = (P("grp", "tile"), P("grp", "tile"), P(("grp", "tile"), None))
    return jax.shard_map(
        shards, mesh=mesh, in_specs=placed, out_specs=P("grp", "tile"), check_vma=False
    )
```

```python
import functools

import jax
import jax.numpy as jnp
from jax import lax
from jax.experimental import pallas as pl
from jax.experimental.pallas import tpu as pltpu
from jax.sharding import PartitionSpec as P

MESH = pl.DeviceIdType.MESH
HIGHEST = lax.Precision.HIGHEST
RD, CD, FAC = 32, 512, 16
N_GRP, N_TILE = 8, 32
HR, HC = 8, 128
ER, EC = RD + 2 * HR, CD + 2 * HC
CO = 64
N_LANE, N_Z = 32, 8
OFFSETS = sorted(
    ((a, b) for a in range(4) for b in range(4)),
    key=lambda o: -(min(o[0], 4 - o[0]) + min(o[1], 4 - o[1])),
)
Z_OFFSETS = (4, 3, 5, 2, 6, 1, 7)
GROUP = 2
HOPS = 5
DIRECTIONS = [(a, b) for a in (-1, 0, 1) for b in (-1, 0, 1) if (a, b) != (0, 0)]


def hops(offset):
    return min(offset[0], 4 - offset[0]) + min(offset[1], 4 - offset[1])


def pick(k, values):
    out = jnp.int32(values[-1])
    for i, value in enumerate(values[:-1]):
        out = jnp.where(k == i, jnp.int32(value), out)
    return out


def beside(field):
    right = pltpu.roll(field, EC - 1, 1)
    left = pltpu.roll(field, 1, 1)
    return right + left + pltpu.roll(field + right, 1, 0) + pltpu.roll(field + left, ER - 1, 0)


def lanes(shape):
    return lax.broadcasted_iota(jnp.int32, shape, len(shape) - 1)


def restricted(block, z_lo):
    top = jnp.sum(block[:FAC], axis=0, keepdims=True)
    low = jnp.sum(block[FAC:], axis=0, keepdims=True)
    sums = jnp.concatenate([top, low, jnp.zeros((6, CD), jnp.float32)], axis=0)
    cell = lax.broadcasted_iota(jnp.int32, (CD, 128), 0) // FAC
    gather = jnp.where(cell == lanes((CD, 128)) % 32, 1.0 / (FAC * FAC), 0.0).astype(jnp.float32)
    means = jnp.dot(sums, gather, precision=HIGHEST, preferred_element_type=jnp.float32)
    lane = lanes((1, 128))
    row = jnp.where((lane // 32) % 2 == 0, means[0:1], means[1:2])
    return jnp.where(lane // 64 == z_lo, row, 0.0)


def spread_columns(rows):
    cell = lax.broadcasted_iota(jnp.int32, (128, CD), 0) % 32
    spread = jnp.where(cell == lanes((128, CD)) // FAC, 1.0, 0.0).astype(jnp.float32)
    return jnp.dot(rows, spread, precision=HIGHEST, preferred_element_type=jnp.float32)


def quarter(row, z_lo, i_hi, valid):
    lane = lanes((1, 128))
    keep = (lane // 32 == z_lo * 2 + i_hi) & valid
    return jnp.where(keep, row, 0.0)


def coarse_neighbours(field):
    sub = lax.broadcasted_iota(jnp.int32, (8, 128), 0)
    lane = lanes((8, 128))
    second = (lane // 32) % 2 == 1
    edge_hi, edge_lo = lane % 32 == 31, lane % 32 == 0
    z_hi_half = lane // 64 == 1
    straight, to_right, to_left = [], [], []
    for c in field:
        fwd = pltpu.roll(c, 32, 1)
        back = pltpu.roll(c, 96, 1)
        above = jnp.where(sub >= 4, pltpu.roll(back, 4, 0), pltpu.roll(back, 5, 0))
        above = jnp.where(sub == 0, 0.0, above)
        below = jnp.where(sub < 4, pltpu.roll(fwd, 4, 0), pltpu.roll(fwd, 3, 0))
        below = jnp.where(sub == 7, 0.0, below)
        up = jnp.where(second, fwd, above)
        down = jnp.where(second, below, back)
        straight.append(31.0 * (up + down))
        to_right.append(31.0 * c + up)
        to_left.append(31.0 * c + down)
    zero = jnp.zeros((8, 128), jnp.float32)
    far_right = [pltpu.roll(v, 95, 1) for v in to_right] + [zero]
    far_left = [zero] + [pltpu.roll(v, 33, 1) for v in to_left]
    total = []
    for i in range(16):
        right = jnp.where(z_hi_half, far_right[i + 1], far_right[i])
        right = jnp.where(edge_hi, right, pltpu.roll(to_right[i], 127, 1))
        left = jnp.where(z_hi_half, far_left[i + 1], far_left[i])
        left = jnp.where(edge_lo, left, pltpu.roll(to_left[i], 1, 1))
        total.append(straight[i] + right + left)
    return total


def column(tile):
    return pl.ds(pl.multiple_of(tile * 128, 128), 128)


def add_products(factor, totals, count, place_of, row_of):
    def step(k, totals):
        xy = place_of(k)
        totals = list(totals)
        for s in range(8):
            row = row_of(xy, s)
            where = column((s % 4) * 32 + (s // 4) * 16 + xy)
            for i in range(8):
                totals[i] = totals[i] + factor[pl.ds(8 * i, 8), where] * row
        return tuple(totals)

    if count == 1:
        return step(0, totals)
    return lax.fori_loop(0, count, step, totals, unroll=4)


def kernel(
    right_ref, diag_ref, factor_ref, out_ref,
    cells, factor, smooth, scale_ref, result,
    row_ref, row_in, chunk_ref, chunk_in, term, term_in, part, part_in,
    fix, fix_in, rhs_ref, last, last_in,
    load_sem, halo_send, halo_recv, send_sem, recv_sem, chunk_sem, fix_sem, last_sem,
):
    g, t = lax.axis_index("grp"), lax.axis_index("tile")
    z_hi, core = lax.div(g, 2), lax.rem(g, 2)
    xy, z_lo = lax.div(t, 2), lax.rem(t, 2)
    x, y = lax.div(xy, 4), lax.rem(xy, 4)
    m, z = core * 16 + xy, z_hi * 2 + z_lo
    rows_in, cols_in = pl.ds(HR, RD), pl.ds(HC, CD)
    xs = [lax.rem(x + a, 4) for a in range(4)]
    ys = [lax.rem(y + b, 4) for b in range(4)]
    zs = [lax.rem(z + c, 8) for c in range(8)]
    mates = [
        (hops(o), (z_hi * 2 + c, xs[o[0]] * 8 + ys[o[1]] * 2 + z_lo))
        for o in OFFSETS[:-1] for c in range(2)
    ]
    mates.append((0, (z_hi * 2 + 1 - core, t)))
    column_mates = [
        (zs[c], (lax.div(zs[c], 2) * 2 + core, xy * 2 + lax.rem(zs[c], 2))) for c in Z_OFFSETS
    ]
    beside_here = [
        (lax.rem(g + a + N_GRP, N_GRP), lax.rem(t + b + N_TILE, N_TILE)) for a, b in DIRECTIONS
    ]

    barrier = pltpu.get_barrier_semaphore()
    for device in [d for _, d in column_mates] + [d for _, d in mates] + beside_here:
        pl.semaphore_signal(barrier, 1, device_id=device, device_id_type=MESH)

    loads = [
        pltpu.make_async_copy(right_ref, cells.at[0, rows_in, cols_in], load_sem.at[0]),
        pltpu.make_async_copy(diag_ref, cells.at[1, rows_in, cols_in], load_sem.at[1]),
        pltpu.make_async_copy(factor_ref, factor, load_sem.at[2]),
    ]
    for load in loads:
        load.start()

    def to_z(stage, source_of, target):
        for there, device in column_mates:
            pltpu.make_async_remote_copy(
                src_ref=source_of(there), dst_ref=target.at[z],
                send_sem=send_sem.at[stage], recv_sem=recv_sem.at[stage],
                device_id=device, device_id_type=MESH,
            ).start()

    def to_m(stage, source, target, near):
        for distance, device in mates:
            pltpu.make_async_remote_copy(
                src_ref=source, dst_ref=target.at[m],
                send_sem=send_sem.at[stage], recv_sem=near.at[distance],
                device_id=device, device_id_type=MESH,
            ).start()

    def arrived(sem, target, count):
        blocks = target.at[pl.ds(0, count)]
        pltpu.make_async_copy(blocks, blocks, sem).wait()

    def arrived_from(near, target, distance):
        arrived(near.at[distance], target, sum(d == distance for d, _ in mates))

    def departed(stage, target, count):
        blocks = target.at[pl.ds(0, count)]
        pltpu.make_async_copy(blocks, blocks, send_sem.at[stage]).wait()

    loads[0].wait()
    row = restricted(cells[0, HR:HR + RD, HC:HC + CD], z_lo)
    row_ref[...] = row
    row_in[z] = row

    pl.semaphore_wait(barrier, N_Z - 1 + N_LANE - 1 + len(DIRECTIONS))
    to_z(0, lambda there: row_ref, row_in)

    loads[1].wait()
    row_from = {-1: HR, 0: HR, 1: RD}
    row_to = {-1: HR + RD, 0: HR, 1: 0}
    row_len = {-1: HR, 0: RD, 1: HR}
    col_from = {-1: HC, 0: HC, 1: CD}
    col_to = {-1: HC + CD, 0: HC, 1: 0}
    col_len = {-1: HC, 0: CD, 1: HC}
    halos = []
    for n, (a, b) in enumerate(DIRECTIONS):
        halos.append(pltpu.make_async_remote_copy(
            src_ref=cells.at[:, pl.ds(row_from[a], row_len[a]), pl.ds(col_from[b], col_len[b])],
            dst_ref=cells.at[:, pl.ds(row_to[a], row_len[a]), pl.ds(col_to[b], col_len[b])],
            send_sem=halo_send.at[n], recv_sem=halo_recv.at[n],
            device_id=beside_here[n],
            device_id_type=MESH,
        ))
        halos[-1].start()

    arrived(recv_sem.at[0], row_in, N_Z - 1)
    chunk = jnp.concatenate([row_in[2 * i] + row_in[2 * i + 1] for i in range(4)], axis=0)
    chunk_ref[...] = chunk
    chunk_in[m] = chunk
    to_m(1, chunk_ref, chunk_in, chunk_sem)

    for halo in halos:
        halo.wait_recv()
    line = g * RD - HR + lax.broadcasted_iota(jnp.int32, (ER, EC), 0)
    place = t * CD - HC + lanes((ER, EC))
    inside = (line >= 0) & (line < N_GRP * RD) & (place >= 0) & (place < N_TILE * CD)
    right_side = cells[0]
    diagonal = cells[1]
    scale = jnp.where(inside, 0.8 / (6.0 + diagonal), 0.0)
    scale_ref[...] = scale
    smoothed = scale * right_side
    for _ in range(3):
        smoothed = 0.2 * smoothed + scale * (right_side + beside(smoothed))
    smooth[...] = smoothed
    left_over = right_side - (6.0 + diagonal) * smoothed + beside(smoothed)
    part[4:5] = restricted(left_over[HR:HR + RD, HC:HC + CD], z_lo)
    part[5:6] = restricted(diagonal[HR:HR + RD, HC:HC + CD], z_lo)
    part[6:8] = jnp.zeros((2, 128), jnp.float32)

    def transposed(inner, store, send):
        inner = [jnp.broadcast_to(v, (8, 128)) for v in inner]

        def term_of(there):
            for h in range(4):
                where = column(h * 32 + there)
                parts = [factor[pl.ds(8 * i, 8), where] * inner[i] for i in range(8)]
                while len(parts) > 1:
                    parts = [parts[i] + parts[i + 1] for i in range(0, len(parts), 2)]
                store(there, h, jnp.sum(parts[0], axis=0, keepdims=True))

        def place_of(k):
            xx = lax.rem(x + pick(k, [o[0] for o in OFFSETS]), 4)
            yy = lax.rem(y + pick(k, [o[1] for o in OFFSETS]), 4)
            return xx * 4 + yy

        def step(j, _):
            ks = [1 + GROUP * j + i for i in range(GROUP)]
            places = [place_of(k) for k in ks]
            for place in places:
                for c in range(2):
                    term_of(c * 16 + place)
            for k, place in zip(ks, places):
                for c in range(2):
                    send(c, place, k)
            return _

        farthest = xs[OFFSETS[0][0]] * 4 + ys[OFFSETS[0][1]]
        for c in range(2):
            term_of(c * 16 + farthest)
            send(c, farthest, 0)
        lax.fori_loop(0, (len(OFFSETS) - 2) // GROUP, step, 0)
        term_of((1 - core) * 16 + xy)
        send(1 - core, xy, len(OFFSETS) - 1)
        term_of(m)

    def store_term(there, h, row):
        term[there, h:h + 1] = row

    def send_term(c, there, k):
        pltpu.make_async_remote_copy(
            src_ref=term.at[c * 16 + there], dst_ref=term_in.at[m],
            send_sem=send_sem.at[2], recv_sem=recv_sem.at[2],
            device_id=(z_hi * 2 + c, there * 2 + z_lo), device_id_type=MESH,
        ).start()

    def store_last(there, h, row):
        last[there, h] = row

    def send_last(c, there, k, places=(*Z_OFFSETS, 0)):
        distance = hops(OFFSETS[k]) if isinstance(k, int) else pick(k, [hops(o) for o in OFFSETS])
        for i, o in enumerate(places):
            half = lax.div(zs[o], 2)
            pltpu.make_async_remote_copy(
                src_ref=last.at[c * 16 + there, half],
                dst_ref=last_in.at[(k * 2 + core) * N_Z + i],
                send_sem=send_sem.at[4], recv_sem=last_sem.at[distance],
                device_id=(half * 2 + c, there * 2 + lax.rem(zs[o], 2)), device_id_type=MESH,
            ).start()

    none = (jnp.zeros((8, 128), jnp.float32),) * 8

    def summed_lanes(totals):
        return [jnp.sum(v, axis=1, keepdims=True) for v in totals]

    loads[2].wait()
    for distance in range(HOPS):
        arrived_from(chunk_sem, chunk_in, distance)
    totals = add_products(
        factor, none, 16, lambda k: k,
        lambda i, s: chunk_in[(s // 4) * 16 + i, s % 4:s % 4 + 1],
    )
    transposed(summed_lanes(totals), store_term, send_term)
    term_in[m] = term[m]

    arrived(recv_sem.at[2], term_in, N_LANE - 1)
    part[0:4] = jnp.sum(term_in[...], axis=0)
    part_in[z] = part[...]
    to_z(3, lambda there: part, part_in)

    arrived(recv_sem.at[3], part_in, N_Z - 1)
    parts = [part_in[i] for i in range(N_Z)]
    coarse = functools.reduce(jnp.add, [v[0:4] for v in parts])
    rest = jnp.concatenate([parts[2 * i][4:5] + parts[2 * i + 1][4:5] for i in range(4)], axis=0)
    mean_diag = jnp.concatenate(
        [parts[2 * i][5:6] + parts[2 * i + 1][5:6] for i in range(4)], axis=0
    )
    own = rest - 0.5 * (126.0 / 256.0 + mean_diag) * coarse
    fix[...] = jnp.where(
        core == 0,
        jnp.concatenate([coarse, own], axis=0),
        jnp.concatenate([own, coarse], axis=0),
    )
    fix_in[m] = fix[...]
    to_m(5, fix, fix_in, fix_sem)

    for distance in range(HOPS):
        arrived_from(fix_sem, fix_in, distance)
    low_rows = lax.broadcasted_iota(jnp.int32, (8, 128), 0) < 4
    field = [jnp.where(low_rows, fix_in[i], fix_in[16 + i]) for i in range(16)]
    around = coarse_neighbours(field)
    for i in range(16):
        own_i = pltpu.roll(jnp.where(low_rows, fix_in[16 + i], fix_in[i]), 4, 0)
        rhs_ref[i] = own_i + (0.5 / 256.0) * around[i]
    totals = add_products(factor, none, 16, lambda k: k, lambda i, s: rhs_ref[i, s:s + 1])
    transposed(summed_lanes(totals), store_last, send_last)
    send_last(core, xy, len(OFFSETS) - 1, Z_OFFSETS)
    last_in[((len(OFFSETS) - 1) * 2 + core) * N_Z + N_Z - 1] = last[m, z_hi]

    def coarse_rows(b):
        tt = t + b
        ok_t = (tt >= 0) & (tt < N_TILE)
        tt = (tt + N_TILE) % N_TILE
        rows = []
        for a, i_hi in ((-1, 1), (0, 0), (0, 1), (1, 0)):
            gg = g + a
            ok = ok_t & (gg >= 0) & (gg < N_GRP)
            gg = (gg + N_GRP) % N_GRP
            row = fix_in[(gg % 2) * 16 + tt // 2, pl.ds((gg % 2) * 4 + gg // 2, 1)]
            rows.append(quarter(row, tt % 2, i_hi, ok))
        return jnp.concatenate(rows + [jnp.zeros((4, 128), jnp.float32)], axis=0)

    lane8 = lanes((8, 128))
    at_left = jnp.sum(jnp.where(lane8 % 32 == 31, coarse_rows(-1), 0.0), axis=1, keepdims=True)
    at_right = jnp.sum(jnp.where(lane8 % 32 == 0, coarse_rows(1), 0.0), axis=1, keepdims=True)
    wide = 0.5 * jnp.concatenate(
        [
            jnp.broadcast_to(at_left, (8, HC)),
            spread_columns(coarse_rows(0)),
            jnp.broadcast_to(at_right, (8, HC)),
        ],
        axis=1,
    )
    fine = jnp.concatenate(
        [
            jnp.broadcast_to(wide[0:1], (HR, EC)),
            jnp.broadcast_to(wide[1:2], (FAC, EC)),
            jnp.broadcast_to(wide[2:3], (FAC, EC)),
            jnp.broadcast_to(wide[3:4], (HR, EC)),
        ],
        axis=0,
    )
    iterate = smooth[...] + fine
    residual = cells[0] - (6.0 + cells[1]) * iterate + beside(iterate)
    scale = scale_ref[...]
    smoothed = scale * residual
    for _ in range(3):
        smoothed = 0.2 * smoothed + scale * (residual + beside(smoothed))
    result[...] = (iterate + smoothed)[HR:HR + RD, HC:HC + CD]

    row = jnp.zeros((1, 128), jnp.float32)
    for distance in range(HOPS):
        places = [k for k, o in enumerate(OFFSETS) if hops(o) == distance]
        first, count = places[0] * 2 * N_Z, len(places) * 2 * N_Z
        arrived(last_sem.at[distance], last_in, count - (distance == 0))
        row = row + jnp.sum(last_in[first:first + count], axis=0)
    pair = jnp.concatenate(
        [quarter(row, z_lo, 0, True), quarter(row, z_lo, 1, True), jnp.zeros((6, 128), jnp.float32)],
        axis=0,
    )
    pair = 0.5 * spread_columns(pair)
    out_ref[:FAC] = result[:FAC] + pair[0:1]
    out_ref[FAC:] = result[FAC:] + pair[1:2]

    for halo in halos:
        halo.wait_send()
    departed(0, row_in, N_Z - 1)
    departed(1, chunk_in, N_LANE - 1)
    departed(2, term_in, N_LANE - 1)
    departed(3, part_in, N_Z - 1)
    departed(5, fix_in, N_LANE - 1)
    departed(4, last_in, N_GRP * N_TILE - 1)


def shards(right_side, diagonal, inverse_factor):
    f32 = jnp.float32
    return pl.pallas_call(
        kernel,
        out_shape=jax.ShapeDtypeStruct((RD, CD), f32),
        in_specs=[pl.BlockSpec(memory_space=pltpu.HBM)] * 3,
        out_specs=pl.BlockSpec(memory_space=pltpu.VMEM),
        scratch_shapes=[
            pltpu.VMEM((2, ER, EC), f32),
            pltpu.VMEM((CO, N_GRP * N_TILE * CO), f32),
            pltpu.VMEM((ER, EC), f32),
            pltpu.VMEM((ER, EC), f32),
            pltpu.VMEM((RD, CD), f32),
            pltpu.VMEM((1, 128), f32),
            pltpu.VMEM((N_Z, 1, 128), f32),
            pltpu.VMEM((4, 128), f32),
            pltpu.VMEM((N_LANE, 4, 128), f32),
            pltpu.VMEM((N_LANE, 4, 128), f32),
            pltpu.VMEM((N_LANE, 4, 128), f32),
            pltpu.VMEM((8, 128), f32),
            pltpu.VMEM((N_Z, 8, 128), f32),
            pltpu.VMEM((8, 128), f32),
            pltpu.VMEM((N_LANE, 8, 128), f32),
            pltpu.VMEM((16, 8, 128), f32),
            pltpu.VMEM((N_LANE, 4, 1, 128), f32),
            pltpu.VMEM((N_GRP * N_TILE, 1, 128), f32),
            pltpu.SemaphoreType.DMA((3,)),
            pltpu.SemaphoreType.DMA((len(DIRECTIONS),)),
            pltpu.SemaphoreType.DMA((len(DIRECTIONS),)),
            pltpu.SemaphoreType.DMA((6,)),
            pltpu.SemaphoreType.DMA((4,)),
            pltpu.SemaphoreType.DMA((HOPS,)),
            pltpu.SemaphoreType.DMA((HOPS,)),
            pltpu.SemaphoreType.DMA((HOPS,)),
        ],
        compiler_params=pltpu.CompilerParams(
            collective_id=0, has_side_effects=True, vmem_limit_bytes=55160 * 1024
        ),
    )(right_side, diagonal, inverse_factor)


def solution(mesh):
    placed = (P("grp", "tile"), P("grp", "tile"), P(("grp", "tile"), None))
    return jax.shard_map(
        shards, mesh=mesh, in_specs=placed, out_specs=P("grp", "tile"), check_vma=False
    )
```

```python
import functools

import jax
import jax.numpy as jnp
from jax import lax
from jax.experimental import pallas as pl
from jax.experimental.pallas import tpu as pltpu
from jax.sharding import PartitionSpec as P

MESH = pl.DeviceIdType.MESH
HIGHEST = lax.Precision.HIGHEST
RD, CD, FAC = 32, 512, 16
N_GRP, N_TILE = 8, 32
HR, HC = 8, 128
ER, EC = RD + 2 * HR, CD + 2 * HC
CO = 64
N_LANE, N_Z = 32, 8
OFFSETS = sorted(
    ((a, b) for a in range(4) for b in range(4)),
    key=lambda o: -(min(o[0], 4 - o[0]) + min(o[1], 4 - o[1])),
)
Z_OFFSETS = (4, 3, 5, 2, 6, 1, 7)
GROUP = 2
HOPS = 5
DIRECTIONS = [(a, b) for a in (-1, 0, 1) for b in (-1, 0, 1) if (a, b) != (0, 0)]


def hops(offset):
    return min(offset[0], 4 - offset[0]) + min(offset[1], 4 - offset[1])


def pick(k, values):
    out = jnp.int32(values[-1])
    for i, value in enumerate(values[:-1]):
        out = jnp.where(k == i, jnp.int32(value), out)
    return out


def beside(field):
    right = pltpu.roll(field, EC - 1, 1)
    left = pltpu.roll(field, 1, 1)
    return right + left + pltpu.roll(field + right, 1, 0) + pltpu.roll(field + left, ER - 1, 0)


def lanes(shape):
    return lax.broadcasted_iota(jnp.int32, shape, len(shape) - 1)


def restricted(block, z_lo):
    top = jnp.sum(block[:FAC], axis=0, keepdims=True)
    low = jnp.sum(block[FAC:], axis=0, keepdims=True)
    sums = jnp.concatenate([top, low, jnp.zeros((6, CD), jnp.float32)], axis=0)
    cell = lax.broadcasted_iota(jnp.int32, (CD, 128), 0) // FAC
    gather = jnp.where(cell == lanes((CD, 128)) % 32, 1.0 / (FAC * FAC), 0.0).astype(jnp.float32)
    means = jnp.dot(sums, gather, precision=HIGHEST, preferred_element_type=jnp.float32)
    lane = lanes((1, 128))
    row = jnp.where((lane // 32) % 2 == 0, means[0:1], means[1:2])
    return jnp.where(lane // 64 == z_lo, row, 0.0)


def spread_columns(rows):
    cell = lax.broadcasted_iota(jnp.int32, (128, CD), 0) % 32
    spread = jnp.where(cell == lanes((128, CD)) // FAC, 1.0, 0.0).astype(jnp.float32)
    return jnp.dot(rows, spread, precision=HIGHEST, preferred_element_type=jnp.float32)


def quarter(row, z_lo, i_hi, valid):
    lane = lanes((1, 128))
    keep = (lane // 32 == z_lo * 2 + i_hi) & valid
    return jnp.where(keep, row, 0.0)


def coarse_neighbours(field):
    sub = lax.broadcasted_iota(jnp.int32, (8, 128), 0)
    lane = lanes((8, 128))
    second = (lane // 32) % 2 == 1
    edge_hi, edge_lo = lane % 32 == 31, lane % 32 == 0
    z_hi_half = lane // 64 == 1
    straight, to_right, to_left = [], [], []
    for c in field:
        fwd = pltpu.roll(c, 32, 1)
        back = pltpu.roll(c, 96, 1)
        above = jnp.where(sub >= 4, pltpu.roll(back, 4, 0), pltpu.roll(back, 5, 0))
        above = jnp.where(sub == 0, 0.0, above)
        below = jnp.where(sub < 4, pltpu.roll(fwd, 4, 0), pltpu.roll(fwd, 3, 0))
        below = jnp.where(sub == 7, 0.0, below)
        up = jnp.where(second, fwd, above)
        down = jnp.where(second, below, back)
        straight.append(31.0 * (up + down))
        to_right.append(31.0 * c + up)
        to_left.append(31.0 * c + down)
    zero = jnp.zeros((8, 128), jnp.float32)
    far_right = [pltpu.roll(v, 95, 1) for v in to_right] + [zero]
    far_left = [zero] + [pltpu.roll(v, 33, 1) for v in to_left]
    total = []
    for i in range(16):
        right = jnp.where(z_hi_half, far_right[i + 1], far_right[i])
        right = jnp.where(edge_hi, right, pltpu.roll(to_right[i], 127, 1))
        left = jnp.where(z_hi_half, far_left[i + 1], far_left[i])
        left = jnp.where(edge_lo, left, pltpu.roll(to_left[i], 1, 1))
        total.append(straight[i] + right + left)
    return total


def column(tile):
    return pl.ds(pl.multiple_of(tile * 128, 128), 128)


def add_products(factor, totals, count, place_of, row_of):
    def step(k, totals):
        xy = place_of(k)
        totals = list(totals)
        for s in range(8):
            row = row_of(xy, s)
            where = column((s % 4) * 32 + (s // 4) * 16 + xy)
            for i in range(8):
                totals[i] = totals[i] + factor[pl.ds(8 * i, 8), where] * row
        return tuple(totals)

    if count == 1:
        return step(0, totals)
    return lax.fori_loop(0, count, step, totals, unroll=4)


def kernel(
    right_ref, diag_ref, factor_ref, out_ref,
    cells, factor, smooth, scale_ref, result,
    row_ref, row_in, chunk_ref, chunk_in, term, term_in, part, part_in,
    fix, fix_in, rhs_ref, last, last_in,
    load_sem, halo_send, halo_recv, send_sem, recv_sem, last_sem,
):
    g, t = lax.axis_index("grp"), lax.axis_index("tile")
    z_hi, core = lax.div(g, 2), lax.rem(g, 2)
    xy, z_lo = lax.div(t, 2), lax.rem(t, 2)
    x, y = lax.div(xy, 4), lax.rem(xy, 4)
    m, z = core * 16 + xy, z_hi * 2 + z_lo
    rows_in, cols_in = pl.ds(HR, RD), pl.ds(HC, CD)
    xs = [lax.rem(x + a, 4) for a in range(4)]
    ys = [lax.rem(y + b, 4) for b in range(4)]
    zs = [lax.rem(z + c, 8) for c in range(8)]
    mates = [
        (z_hi * 2 + c, xs[o[0]] * 8 + ys[o[1]] * 2 + z_lo)
        for o in OFFSETS[:-1] for c in range(2)
    ]
    mates.append((z_hi * 2 + 1 - core, t))
    column_mates = [
        (zs[c], (lax.div(zs[c], 2) * 2 + core, xy * 2 + lax.rem(zs[c], 2))) for c in Z_OFFSETS
    ]
    beside_here = [
        (lax.rem(g + a + N_GRP, N_GRP), lax.rem(t + b + N_TILE, N_TILE)) for a, b in DIRECTIONS
    ]

    barrier = pltpu.get_barrier_semaphore()
    for device in [d for _, d in column_mates] + mates + beside_here:
        pl.semaphore_signal(barrier, 1, device_id=device, device_id_type=MESH)

    loads = [
        pltpu.make_async_copy(right_ref, cells.at[0, rows_in, cols_in], load_sem.at[0]),
        pltpu.make_async_copy(diag_ref, cells.at[1, rows_in, cols_in], load_sem.at[1]),
        pltpu.make_async_copy(factor_ref, factor, load_sem.at[2]),
    ]
    for load in loads:
        load.start()

    def to_z(stage, source_of, target):
        for there, device in column_mates:
            pltpu.make_async_remote_copy(
                src_ref=source_of(there), dst_ref=target.at[z],
                send_sem=send_sem.at[stage], recv_sem=recv_sem.at[stage],
                device_id=device, device_id_type=MESH,
            ).start()

    def to_m(stage, source, target):
        for device in mates:
            pltpu.make_async_remote_copy(
                src_ref=source, dst_ref=target.at[m],
                send_sem=send_sem.at[stage], recv_sem=recv_sem.at[stage],
                device_id=device, device_id_type=MESH,
            ).start()

    def arrived(sem, target, count):
        blocks = target.at[pl.ds(0, count)]
        pltpu.make_async_copy(blocks, blocks, sem).wait()

    def departed(stage, target, count):
        blocks = target.at[pl.ds(0, count)]
        pltpu.make_async_copy(blocks, blocks, send_sem.at[stage]).wait()

    loads[0].wait()
    row = restricted(cells[0, HR:HR + RD, HC:HC + CD], z_lo)
    row_ref[...] = row
    row_in[z] = row

    pl.semaphore_wait(barrier, N_Z - 1 + N_LANE - 1 + len(DIRECTIONS))
    to_z(0, lambda there: row_ref, row_in)

    loads[1].wait()
    row_from = {-1: HR, 0: HR, 1: RD}
    row_to = {-1: HR + RD, 0: HR, 1: 0}
    row_len = {-1: HR, 0: RD, 1: HR}
    col_from = {-1: HC, 0: HC, 1: CD}
    col_to = {-1: HC + CD, 0: HC, 1: 0}
    col_len = {-1: HC, 0: CD, 1: HC}
    halos = []
    for n, (a, b) in enumerate(DIRECTIONS):
        halos.append(pltpu.make_async_remote_copy(
            src_ref=cells.at[:, pl.ds(row_from[a], row_len[a]), pl.ds(col_from[b], col_len[b])],
            dst_ref=cells.at[:, pl.ds(row_to[a], row_len[a]), pl.ds(col_to[b], col_len[b])],
            send_sem=halo_send.at[n], recv_sem=halo_recv.at[n],
            device_id=beside_here[n],
            device_id_type=MESH,
        ))
        halos[-1].start()

    arrived(recv_sem.at[0], row_in, N_Z - 1)
    chunk = jnp.concatenate([row_in[2 * i] + row_in[2 * i + 1] for i in range(4)], axis=0)
    chunk_ref[...] = chunk
    chunk_in[m] = chunk
    to_m(1, chunk_ref, chunk_in)

    for halo in halos:
        halo.wait_recv()
    line = g * RD - HR + lax.broadcasted_iota(jnp.int32, (ER, EC), 0)
    place = t * CD - HC + lanes((ER, EC))
    inside = (line >= 0) & (line < N_GRP * RD) & (place >= 0) & (place < N_TILE * CD)
    right_side = cells[0]
    diagonal = cells[1]
    scale = jnp.where(inside, 0.8 / (6.0 + diagonal), 0.0)
    scale_ref[...] = scale
    smoothed = scale * right_side
    for _ in range(3):
        smoothed = 0.2 * smoothed + scale * (right_side + beside(smoothed))
    smooth[...] = smoothed
    left_over = right_side - (6.0 + diagonal) * smoothed + beside(smoothed)
    part[4:5] = restricted(left_over[HR:HR + RD, HC:HC + CD], z_lo)
    part[5:6] = restricted(diagonal[HR:HR + RD, HC:HC + CD], z_lo)
    part[6:8] = jnp.zeros((2, 128), jnp.float32)

    def transposed(inner, store, send):
        inner = [jnp.broadcast_to(v, (8, 128)) for v in inner]

        def term_of(there):
            for h in range(4):
                where = column(h * 32 + there)
                parts = [factor[pl.ds(8 * i, 8), where] * inner[i] for i in range(8)]
                while len(parts) > 1:
                    parts = [parts[i] + parts[i + 1] for i in range(0, len(parts), 2)]
                store(there, h, jnp.sum(parts[0], axis=0, keepdims=True))

        def place_of(k):
            xx = lax.rem(x + pick(k, [o[0] for o in OFFSETS]), 4)
            yy = lax.rem(y + pick(k, [o[1] for o in OFFSETS]), 4)
            return xx * 4 + yy

        def step(j, _):
            ks = [1 + GROUP * j + i for i in range(GROUP)]
            places = [place_of(k) for k in ks]
            for place in places:
                for c in range(2):
                    term_of(c * 16 + place)
            for k, place in zip(ks, places):
                for c in range(2):
                    send(c, place, k)
            return _

        farthest = xs[OFFSETS[0][0]] * 4 + ys[OFFSETS[0][1]]
        for c in range(2):
            term_of(c * 16 + farthest)
            send(c, farthest, 0)
        lax.fori_loop(0, (len(OFFSETS) - 2) // GROUP, step, 0)
        term_of((1 - core) * 16 + xy)
        send(1 - core, xy, len(OFFSETS) - 1)
        term_of(m)

    def store_term(there, h, row):
        term[there, h:h + 1] = row

    def send_term(c, there, k):
        pltpu.make_async_remote_copy(
            src_ref=term.at[c * 16 + there], dst_ref=term_in.at[m],
            send_sem=send_sem.at[2], recv_sem=recv_sem.at[2],
            device_id=(z_hi * 2 + c, there * 2 + z_lo), device_id_type=MESH,
        ).start()

    def store_last(there, h, row):
        last[there, h] = row

    def send_last(c, there, k, places=(*Z_OFFSETS, 0)):
        distance = hops(OFFSETS[k]) if isinstance(k, int) else pick(k, [hops(o) for o in OFFSETS])
        for i, o in enumerate(places):
            half = lax.div(zs[o], 2)
            pltpu.make_async_remote_copy(
                src_ref=last.at[c * 16 + there, half],
                dst_ref=last_in.at[(k * 2 + core) * N_Z + i],
                send_sem=send_sem.at[4], recv_sem=last_sem.at[distance],
                device_id=(half * 2 + c, there * 2 + lax.rem(zs[o], 2)), device_id_type=MESH,
            ).start()

    none = (jnp.zeros((8, 128), jnp.float32),) * 8

    def summed_lanes(totals):
        return [jnp.sum(v, axis=1, keepdims=True) for v in totals]

    loads[2].wait()
    arrived(recv_sem.at[1], chunk_in, N_LANE - 1)
    totals = add_products(
        factor, none, 16, lambda k: k,
        lambda i, s: chunk_in[(s // 4) * 16 + i, s % 4:s % 4 + 1],
    )
    transposed(summed_lanes(totals), store_term, send_term)
    term_in[m] = term[m]

    arrived(recv_sem.at[2], term_in, N_LANE - 1)
    part[0:4] = jnp.sum(term_in[...], axis=0)
    part_in[z] = part[...]
    to_z(3, lambda there: part, part_in)

    arrived(recv_sem.at[3], part_in, N_Z - 1)
    parts = [part_in[i] for i in range(N_Z)]
    coarse = functools.reduce(jnp.add, [v[0:4] for v in parts])
    rest = jnp.concatenate([parts[2 * i][4:5] + parts[2 * i + 1][4:5] for i in range(4)], axis=0)
    mean_diag = jnp.concatenate(
        [parts[2 * i][5:6] + parts[2 * i + 1][5:6] for i in range(4)], axis=0
    )
    own = rest - 0.5 * (126.0 / 256.0 + mean_diag) * coarse
    fix[...] = jnp.where(
        core == 0,
        jnp.concatenate([coarse, own], axis=0),
        jnp.concatenate([own, coarse], axis=0),
    )
    fix_in[m] = fix[...]
    to_m(5, fix, fix_in)

    arrived(recv_sem.at[5], fix_in, N_LANE - 1)
    low_rows = lax.broadcasted_iota(jnp.int32, (8, 128), 0) < 4
    field = [jnp.where(low_rows, fix_in[i], fix_in[16 + i]) for i in range(16)]
    around = coarse_neighbours(field)
    for i in range(16):
        own_i = pltpu.roll(jnp.where(low_rows, fix_in[16 + i], fix_in[i]), 4, 0)
        rhs_ref[i] = own_i + (0.5 / 256.0) * around[i]
    totals = add_products(factor, none, 16, lambda k: k, lambda i, s: rhs_ref[i, s:s + 1])
    transposed(summed_lanes(totals), store_last, send_last)
    send_last(core, xy, len(OFFSETS) - 1, Z_OFFSETS)
    last_in[((len(OFFSETS) - 1) * 2 + core) * N_Z + N_Z - 1] = last[m, z_hi]

    def coarse_rows(b):
        tt = t + b
        ok_t = (tt >= 0) & (tt < N_TILE)
        tt = (tt + N_TILE) % N_TILE
        rows = []
        for a, i_hi in ((-1, 1), (0, 0), (0, 1), (1, 0)):
            gg = g + a
            ok = ok_t & (gg >= 0) & (gg < N_GRP)
            gg = (gg + N_GRP) % N_GRP
            row = fix_in[(gg % 2) * 16 + tt // 2, pl.ds((gg % 2) * 4 + gg // 2, 1)]
            rows.append(quarter(row, tt % 2, i_hi, ok))
        return jnp.concatenate(rows + [jnp.zeros((4, 128), jnp.float32)], axis=0)

    lane8 = lanes((8, 128))
    at_left = jnp.sum(jnp.where(lane8 % 32 == 31, coarse_rows(-1), 0.0), axis=1, keepdims=True)
    at_right = jnp.sum(jnp.where(lane8 % 32 == 0, coarse_rows(1), 0.0), axis=1, keepdims=True)
    wide = 0.5 * jnp.concatenate(
        [
            jnp.broadcast_to(at_left, (8, HC)),
            spread_columns(coarse_rows(0)),
            jnp.broadcast_to(at_right, (8, HC)),
        ],
        axis=1,
    )
    fine = jnp.concatenate(
        [
            jnp.broadcast_to(wide[0:1], (HR, EC)),
            jnp.broadcast_to(wide[1:2], (FAC, EC)),
            jnp.broadcast_to(wide[2:3], (FAC, EC)),
            jnp.broadcast_to(wide[3:4], (HR, EC)),
        ],
        axis=0,
    )
    iterate = smooth[...] + fine
    residual = cells[0] - (6.0 + cells[1]) * iterate + beside(iterate)
    scale = scale_ref[...]
    smoothed = scale * residual
    for _ in range(3):
        smoothed = 0.2 * smoothed + scale * (residual + beside(smoothed))
    result[...] = (iterate + smoothed)[HR:HR + RD, HC:HC + CD]

    for halo in halos:
        halo.wait_send()
    departed(0, row_in, N_Z - 1)
    departed(1, chunk_in, N_LANE - 1)
    departed(2, term_in, N_LANE - 1)
    departed(3, part_in, N_Z - 1)
    departed(5, fix_in, N_LANE - 1)

    row = jnp.zeros((1, 128), jnp.float32)
    for distance in range(HOPS):
        places = [k for k, o in enumerate(OFFSETS) if hops(o) == distance]
        first, count = places[0] * 2 * N_Z, len(places) * 2 * N_Z
        arrived(last_sem.at[distance], last_in, count - (distance == 0))
        row = row + jnp.sum(last_in[first:first + count], axis=0)
    pair = jnp.concatenate(
        [quarter(row, z_lo, 0, True), quarter(row, z_lo, 1, True), jnp.zeros((6, 128), jnp.float32)],
        axis=0,
    )
    pair = 0.5 * spread_columns(pair)
    out_ref[:FAC] = result[:FAC] + pair[0:1]
    out_ref[FAC:] = result[FAC:] + pair[1:2]

    departed(4, last_in, N_GRP * N_TILE - 1)


def shards(right_side, diagonal, inverse_factor):
    f32 = jnp.float32
    return pl.pallas_call(
        kernel,
        out_shape=jax.ShapeDtypeStruct((RD, CD), f32),
        in_specs=[pl.BlockSpec(memory_space=pltpu.HBM)] * 3,
        out_specs=pl.BlockSpec(memory_space=pltpu.VMEM),
        scratch_shapes=[
            pltpu.VMEM((2, ER, EC), f32),
            pltpu.VMEM((CO, N_GRP * N_TILE * CO), f32),
            pltpu.VMEM((ER, EC), f32),
            pltpu.VMEM((ER, EC), f32),
            pltpu.VMEM((RD, CD), f32),
            pltpu.VMEM((1, 128), f32),
            pltpu.VMEM((N_Z, 1, 128), f32),
            pltpu.VMEM((4, 128), f32),
            pltpu.VMEM((N_LANE, 4, 128), f32),
            pltpu.VMEM((N_LANE, 4, 128), f32),
            pltpu.VMEM((N_LANE, 4, 128), f32),
            pltpu.VMEM((8, 128), f32),
            pltpu.VMEM((N_Z, 8, 128), f32),
            pltpu.VMEM((8, 128), f32),
            pltpu.VMEM((N_LANE, 8, 128), f32),
            pltpu.VMEM((16, 8, 128), f32),
            pltpu.VMEM((N_LANE, 4, 1, 128), f32),
            pltpu.VMEM((N_GRP * N_TILE, 1, 128), f32),
            pltpu.SemaphoreType.DMA((3,)),
            pltpu.SemaphoreType.DMA((len(DIRECTIONS),)),
            pltpu.SemaphoreType.DMA((len(DIRECTIONS),)),
            pltpu.SemaphoreType.DMA((6,)),
            pltpu.SemaphoreType.DMA((6,)),
            pltpu.SemaphoreType.DMA((HOPS,)),
        ],
        compiler_params=pltpu.CompilerParams(
            collective_id=0, has_side_effects=True, vmem_limit_bytes=55160 * 1024
        ),
    )(right_side, diagonal, inverse_factor)


def solution(mesh):
    placed = (P("grp", "tile"), P("grp", "tile"), P(("grp", "tile"), None))
    return jax.shard_map(
        shards, mesh=mesh, in_specs=placed, out_specs=P("grp", "tile"), check_vma=False
    )
```

```python
import functools

import jax
import jax.numpy as jnp
from jax import lax
from jax.experimental import pallas as pl
from jax.experimental.pallas import tpu as pltpu
from jax.sharding import PartitionSpec as P

MESH = pl.DeviceIdType.MESH
HIGHEST = lax.Precision.HIGHEST
RD, CD, FAC = 32, 512, 16
N_GRP, N_TILE = 8, 32
HR, HC = 8, 128
ER, EC = RD + 2 * HR, CD + 2 * HC
CO = 64
N_LANE, N_Z = 32, 8
OFFSETS = sorted(
    ((a, b) for a in range(4) for b in range(4)),
    key=lambda o: -(min(o[0], 4 - o[0]) + min(o[1], 4 - o[1])),
)
Z_OFFSETS = (4, 3, 5, 2, 6, 1, 7)
GROUP = 2
HOPS = 5
DIRECTIONS = [(a, b) for a in (-1, 0, 1) for b in (-1, 0, 1) if (a, b) != (0, 0)]


def hops(offset):
    return min(offset[0], 4 - offset[0]) + min(offset[1], 4 - offset[1])


def pick(k, values):
    out = jnp.int32(values[-1])
    for i, value in enumerate(values[:-1]):
        out = jnp.where(k == i, jnp.int32(value), out)
    return out


def beside(field):
    right = pltpu.roll(field, EC - 1, 1)
    left = pltpu.roll(field, 1, 1)
    return right + left + pltpu.roll(field + right, 1, 0) + pltpu.roll(field + left, ER - 1, 0)


def lanes(shape):
    return lax.broadcasted_iota(jnp.int32, shape, len(shape) - 1)


def restricted(block, z_lo):
    top = jnp.sum(block[:FAC], axis=0, keepdims=True)
    low = jnp.sum(block[FAC:], axis=0, keepdims=True)
    sums = jnp.concatenate([top, low, jnp.zeros((6, CD), jnp.float32)], axis=0)
    cell = lax.broadcasted_iota(jnp.int32, (CD, 128), 0) // FAC
    gather = jnp.where(cell == lanes((CD, 128)) % 32, 1.0 / (FAC * FAC), 0.0).astype(jnp.float32)
    means = jnp.dot(sums, gather, precision=HIGHEST, preferred_element_type=jnp.float32)
    lane = lanes((1, 128))
    row = jnp.where((lane // 32) % 2 == 0, means[0:1], means[1:2])
    return jnp.where(lane // 64 == z_lo, row, 0.0)


def spread_columns(rows):
    cell = lax.broadcasted_iota(jnp.int32, (128, CD), 0) % 32
    spread = jnp.where(cell == lanes((128, CD)) // FAC, 1.0, 0.0).astype(jnp.float32)
    return jnp.dot(rows, spread, precision=HIGHEST, preferred_element_type=jnp.float32)


def quarter(row, z_lo, i_hi, valid):
    lane = lanes((1, 128))
    keep = (lane // 32 == z_lo * 2 + i_hi) & valid
    return jnp.where(keep, row, 0.0)


def coarse_neighbours(field):
    sub = lax.broadcasted_iota(jnp.int32, (8, 128), 0)
    lane = lanes((8, 128))
    second = (lane // 32) % 2 == 1
    edge_hi, edge_lo = lane % 32 == 31, lane % 32 == 0
    z_hi_half = lane // 64 == 1
    straight, to_right, to_left = [], [], []
    for c in field:
        fwd = pltpu.roll(c, 32, 1)
        back = pltpu.roll(c, 96, 1)
        above = jnp.where(sub >= 4, pltpu.roll(back, 4, 0), pltpu.roll(back, 5, 0))
        above = jnp.where(sub == 0, 0.0, above)
        below = jnp.where(sub < 4, pltpu.roll(fwd, 4, 0), pltpu.roll(fwd, 3, 0))
        below = jnp.where(sub == 7, 0.0, below)
        up = jnp.where(second, fwd, above)
        down = jnp.where(second, below, back)
        straight.append(31.0 * (up + down))
        to_right.append(31.0 * c + up)
        to_left.append(31.0 * c + down)
    zero = jnp.zeros((8, 128), jnp.float32)
    far_right = [pltpu.roll(v, 95, 1) for v in to_right] + [zero]
    far_left = [zero] + [pltpu.roll(v, 33, 1) for v in to_left]
    total = []
    for i in range(16):
        right = jnp.where(z_hi_half, far_right[i + 1], far_right[i])
        right = jnp.where(edge_hi, right, pltpu.roll(to_right[i], 127, 1))
        left = jnp.where(z_hi_half, far_left[i + 1], far_left[i])
        left = jnp.where(edge_lo, left, pltpu.roll(to_left[i], 1, 1))
        total.append(straight[i] + right + left)
    return total


def column(tile):
    return pl.ds(pl.multiple_of(tile * 128, 128), 128)


def add_products(factor, totals, count, place_of, row_of):
    def step(k, totals):
        xy = place_of(k)
        totals = list(totals)
        for s in range(8):
            row = row_of(xy, s)
            where = column((s % 4) * 32 + (s // 4) * 16 + xy)
            for i in range(8):
                totals[i] = totals[i] + factor[pl.ds(8 * i, 8), where] * row
        return tuple(totals)

    if count == 1:
        return step(0, totals)
    return lax.fori_loop(0, count, step, totals, unroll=4)


def kernel(
    right_ref, diag_ref, factor_ref, out_ref,
    cells, factor, smooth, scale_ref, result,
    row_ref, row_in, chunk_ref, chunk_in, term, term_in, part, part_in,
    side, side_in, side_chunk, side_all, fix, fix_in, rhs_ref, weight_ref, last, last_in,
    load_sem, halo_send, halo_recv, send_sem, recv_sem, last_sem,
):
    g, t = lax.axis_index("grp"), lax.axis_index("tile")
    z_hi, core = lax.div(g, 2), lax.rem(g, 2)
    xy, z_lo = lax.div(t, 2), lax.rem(t, 2)
    x, y = lax.div(xy, 4), lax.rem(xy, 4)
    m, z = core * 16 + xy, z_hi * 2 + z_lo
    rows_in, cols_in = pl.ds(HR, RD), pl.ds(HC, CD)
    xs = [lax.rem(x + a, 4) for a in range(4)]
    ys = [lax.rem(y + b, 4) for b in range(4)]
    zs = [lax.rem(z + c, 8) for c in range(8)]
    mates = [
        (z_hi * 2 + c, xs[o[0]] * 8 + ys[o[1]] * 2 + z_lo)
        for o in OFFSETS[:-1] for c in range(2)
    ]
    mates.append((z_hi * 2 + 1 - core, t))
    column_mates = [
        (zs[c], (lax.div(zs[c], 2) * 2 + core, xy * 2 + lax.rem(zs[c], 2))) for c in Z_OFFSETS
    ]
    beside_here = [
        (lax.rem(g + a + N_GRP, N_GRP), lax.rem(t + b + N_TILE, N_TILE)) for a, b in DIRECTIONS
    ]

    barrier = pltpu.get_barrier_semaphore()
    for device in [d for _, d in column_mates] + mates + beside_here:
        pl.semaphore_signal(barrier, 1, device_id=device, device_id_type=MESH)

    loads = [
        pltpu.make_async_copy(right_ref, cells.at[0, rows_in, cols_in], load_sem.at[0]),
        pltpu.make_async_copy(diag_ref, cells.at[1, rows_in, cols_in], load_sem.at[1]),
        pltpu.make_async_copy(factor_ref, factor, load_sem.at[2]),
    ]
    for load in loads:
        load.start()

    def to_z(stage, source_of, target):
        for there, device in column_mates:
            pltpu.make_async_remote_copy(
                src_ref=source_of(there), dst_ref=target.at[z],
                send_sem=send_sem.at[stage], recv_sem=recv_sem.at[stage],
                device_id=device, device_id_type=MESH,
            ).start()

    def to_m(stage, source, target):
        for device in mates:
            pltpu.make_async_remote_copy(
                src_ref=source, dst_ref=target.at[m],
                send_sem=send_sem.at[stage], recv_sem=recv_sem.at[stage],
                device_id=device, device_id_type=MESH,
            ).start()

    def arrived(sem, target, count):
        blocks = target.at[pl.ds(0, count)]
        pltpu.make_async_copy(blocks, blocks, sem).wait()

    def departed(stage, target, count):
        blocks = target.at[pl.ds(0, count)]
        pltpu.make_async_copy(blocks, blocks, send_sem.at[stage]).wait()

    loads[0].wait()
    row = restricted(cells[0, HR:HR + RD, HC:HC + CD], z_lo)
    row_ref[...] = row
    row_in[z] = row

    pl.semaphore_wait(barrier, N_Z - 1 + N_LANE - 1 + len(DIRECTIONS))
    to_z(0, lambda there: row_ref, row_in)

    loads[1].wait()
    row_from = {-1: HR, 0: HR, 1: RD}
    row_to = {-1: HR + RD, 0: HR, 1: 0}
    row_len = {-1: HR, 0: RD, 1: HR}
    col_from = {-1: HC, 0: HC, 1: CD}
    col_to = {-1: HC + CD, 0: HC, 1: 0}
    col_len = {-1: HC, 0: CD, 1: HC}
    halos = []
    for n, (a, b) in enumerate(DIRECTIONS):
        halos.append(pltpu.make_async_remote_copy(
            src_ref=cells.at[:, pl.ds(row_from[a], row_len[a]), pl.ds(col_from[b], col_len[b])],
            dst_ref=cells.at[:, pl.ds(row_to[a], row_len[a]), pl.ds(col_to[b], col_len[b])],
            send_sem=halo_send.at[n], recv_sem=halo_recv.at[n],
            device_id=beside_here[n],
            device_id_type=MESH,
        ))
        halos[-1].start()

    arrived(recv_sem.at[0], row_in, N_Z - 1)
    chunk = jnp.concatenate([row_in[2 * i] + row_in[2 * i + 1] for i in range(4)], axis=0)
    chunk_ref[...] = chunk
    chunk_in[m] = chunk
    to_m(1, chunk_ref, chunk_in)

    for halo in halos:
        halo.wait_recv()
    line = g * RD - HR + lax.broadcasted_iota(jnp.int32, (ER, EC), 0)
    place = t * CD - HC + lanes((ER, EC))
    inside = (line >= 0) & (line < N_GRP * RD) & (place >= 0) & (place < N_TILE * CD)
    right_side = cells[0]
    diagonal = cells[1]
    scale = jnp.where(inside, 0.8 / (6.0 + diagonal), 0.0)
    scale_ref[...] = scale
    smoothed = scale * right_side
    for _ in range(3):
        smoothed = 0.2 * smoothed + scale * (right_side + beside(smoothed))
    smooth[...] = smoothed
    left_over = right_side - (6.0 + diagonal) * smoothed + beside(smoothed)
    side[0:1] = restricted(left_over[HR:HR + RD, HC:HC + CD], z_lo)
    side[1:2] = restricted(diagonal[HR:HR + RD, HC:HC + CD], z_lo)
    side_in[z] = side[...]
    to_z(6, lambda there: side, side_in)

    def transposed(inner, store, send):
        inner = [jnp.broadcast_to(v, (8, 128)) for v in inner]

        def term_of(there):
            for h in range(4):
                where = column(h * 32 + there)
                parts = [factor[pl.ds(8 * i, 8), where] * inner[i] for i in range(8)]
                while len(parts) > 1:
                    parts = [parts[i] + parts[i + 1] for i in range(0, len(parts), 2)]
                store(there, h, jnp.sum(parts[0], axis=0, keepdims=True))

        def place_of(k):
            xx = lax.rem(x + pick(k, [o[0] for o in OFFSETS]), 4)
            yy = lax.rem(y + pick(k, [o[1] for o in OFFSETS]), 4)
            return xx * 4 + yy

        def step(j, _):
            ks = [1 + GROUP * j + i for i in range(GROUP)]
            places = [place_of(k) for k in ks]
            for place in places:
                for c in range(2):
                    term_of(c * 16 + place)
            for k, place in zip(ks, places):
                for c in range(2):
                    send(c, place, k)
            return _

        farthest = xs[OFFSETS[0][0]] * 4 + ys[OFFSETS[0][1]]
        for c in range(2):
            term_of(c * 16 + farthest)
            send(c, farthest, 0)
        lax.fori_loop(0, (len(OFFSETS) - 2) // GROUP, step, 0)
        term_of((1 - core) * 16 + xy)
        send(1 - core, xy, len(OFFSETS) - 1)
        term_of(m)

    def store_term(there, h, row):
        term[there, h:h + 1] = row

    def send_term(c, there, k):
        pltpu.make_async_remote_copy(
            src_ref=term.at[c * 16 + there], dst_ref=term_in.at[m],
            send_sem=send_sem.at[2], recv_sem=recv_sem.at[2],
            device_id=(z_hi * 2 + c, there * 2 + z_lo), device_id_type=MESH,
        ).start()

    def store_last(there, h, row):
        last[there, h] = row

    def send_last(c, there, k, places=(*Z_OFFSETS, 0)):
        distance = hops(OFFSETS[k]) if isinstance(k, int) else pick(k, [hops(o) for o in OFFSETS])
        for i, o in enumerate(places):
            half = lax.div(zs[o], 2)
            pltpu.make_async_remote_copy(
                src_ref=last.at[c * 16 + there, half],
                dst_ref=last_in.at[(k * 2 + core) * N_Z + i],
                send_sem=send_sem.at[4], recv_sem=last_sem.at[distance],
                device_id=(half * 2 + c, there * 2 + lax.rem(zs[o], 2)), device_id_type=MESH,
            ).start()

    none = (jnp.zeros((8, 128), jnp.float32),) * 8

    def summed_lanes(totals):
        return [jnp.sum(v, axis=1, keepdims=True) for v in totals]

    loads[2].wait()
    arrived(recv_sem.at[1], chunk_in, N_LANE - 1)
    totals = add_products(
        factor, none, 16, lambda k: k,
        lambda i, s: chunk_in[(s // 4) * 16 + i, s % 4:s % 4 + 1],
    )
    transposed(summed_lanes(totals), store_term, send_term)
    term_in[m] = term[m]

    arrived(recv_sem.at[6], side_in, N_Z - 1)
    rest, mean_diag = (
        jnp.concatenate(
            [side_in[2 * i][r:r + 1] + side_in[2 * i + 1][r:r + 1] for i in range(4)], axis=0
        )
        for r in range(2)
    )
    side_chunk[...] = jnp.where(
        core == 0,
        jnp.concatenate([rest, mean_diag], axis=0),
        jnp.concatenate([mean_diag, rest], axis=0),
    )
    side_all[m] = side_chunk[...]
    to_m(7, side_chunk, side_all)

    arrived(recv_sem.at[2], term_in, N_LANE - 1)
    part[...] = jnp.sum(term_in[...], axis=0)
    part_in[z] = part[...]
    to_z(3, lambda there: part, part_in)

    low_rows = lax.broadcasted_iota(jnp.int32, (8, 128), 0) < 4
    arrived(recv_sem.at[7], side_all, N_LANE - 1)
    for i in range(16):
        low, high = side_all[i], side_all[16 + i]
        rhs_ref[i] = jnp.where(low_rows, low, high)
        weight_ref[i] = 0.5 * (126.0 / 256.0 + pltpu.roll(jnp.where(low_rows, high, low), 4, 0))

    arrived(recv_sem.at[3], part_in, N_Z - 1)
    fix[...] = functools.reduce(jnp.add, [part_in[i] for i in range(N_Z)])
    fix_in[m] = fix[...]
    to_m(5, fix, fix_in)

    arrived(recv_sem.at[5], fix_in, N_LANE - 1)
    field = [jnp.concatenate([fix_in[i], fix_in[16 + i]], axis=0) for i in range(16)]
    around = coarse_neighbours(field)
    for i in range(16):
        rhs_ref[i] = rhs_ref[i] - weight_ref[i] * field[i] + (0.5 / 256.0) * around[i]
    totals = add_products(factor, none, 16, lambda k: k, lambda i, s: rhs_ref[i, s:s + 1])
    transposed(summed_lanes(totals), store_last, send_last)
    send_last(core, xy, len(OFFSETS) - 1, Z_OFFSETS)
    last_in[((len(OFFSETS) - 1) * 2 + core) * N_Z + N_Z - 1] = last[m, z_hi]

    def coarse_rows(b):
        tt = t + b
        ok_t = (tt >= 0) & (tt < N_TILE)
        tt = (tt + N_TILE) % N_TILE
        rows = []
        for a, i_hi in ((-1, 1), (0, 0), (0, 1), (1, 0)):
            gg = g + a
            ok = ok_t & (gg >= 0) & (gg < N_GRP)
            gg = (gg + N_GRP) % N_GRP
            row = fix_in[(gg % 2) * 16 + tt // 2, pl.ds(gg // 2, 1)]
            rows.append(quarter(row, tt % 2, i_hi, ok))
        return jnp.concatenate(rows + [jnp.zeros((4, 128), jnp.float32)], axis=0)

    lane8 = lanes((8, 128))
    at_left = jnp.sum(jnp.where(lane8 % 32 == 31, coarse_rows(-1), 0.0), axis=1, keepdims=True)
    at_right = jnp.sum(jnp.where(lane8 % 32 == 0, coarse_rows(1), 0.0), axis=1, keepdims=True)
    wide = 0.5 * jnp.concatenate(
        [
            jnp.broadcast_to(at_left, (8, HC)),
            spread_columns(coarse_rows(0)),
            jnp.broadcast_to(at_right, (8, HC)),
        ],
        axis=1,
    )
    fine = jnp.concatenate(
        [
            jnp.broadcast_to(wide[0:1], (HR, EC)),
            jnp.broadcast_to(wide[1:2], (FAC, EC)),
            jnp.broadcast_to(wide[2:3], (FAC, EC)),
            jnp.broadcast_to(wide[3:4], (HR, EC)),
        ],
        axis=0,
    )
    iterate = smooth[...] + fine
    residual = cells[0] - (6.0 + cells[1]) * iterate + beside(iterate)
    scale = scale_ref[...]
    smoothed = scale * residual
    for _ in range(3):
        smoothed = 0.2 * smoothed + scale * (residual + beside(smoothed))
    result[...] = (iterate + smoothed)[HR:HR + RD, HC:HC + CD]

    for halo in halos:
        halo.wait_send()
    departed(0, row_in, N_Z - 1)
    departed(1, chunk_in, N_LANE - 1)
    departed(2, term_in, N_LANE - 1)
    departed(3, part_in, N_Z - 1)
    departed(6, side_in, N_Z - 1)
    departed(7, side_all, N_LANE - 1)
    departed(5, fix_in, N_LANE - 1)

    row = jnp.zeros((1, 128), jnp.float32)
    for distance in range(HOPS):
        places = [k for k, o in enumerate(OFFSETS) if hops(o) == distance]
        first, count = places[0] * 2 * N_Z, len(places) * 2 * N_Z
        arrived(last_sem.at[distance], last_in, count - (distance == 0))
        row = row + jnp.sum(last_in[first:first + count], axis=0)
    pair = jnp.concatenate(
        [quarter(row, z_lo, 0, True), quarter(row, z_lo, 1, True), jnp.zeros((6, 128), jnp.float32)],
        axis=0,
    )
    pair = 0.5 * spread_columns(pair)
    out_ref[:FAC] = result[:FAC] + pair[0:1]
    out_ref[FAC:] = result[FAC:] + pair[1:2]

    departed(4, last_in, N_GRP * N_TILE - 1)


def shards(right_side, diagonal, inverse_factor):
    f32 = jnp.float32
    return pl.pallas_call(
        kernel,
        out_shape=jax.ShapeDtypeStruct((RD, CD), f32),
        in_specs=[pl.BlockSpec(memory_space=pltpu.HBM)] * 3,
        out_specs=pl.BlockSpec(memory_space=pltpu.VMEM),
        scratch_shapes=[
            pltpu.VMEM((2, ER, EC), f32),
            pltpu.VMEM((CO, N_GRP * N_TILE * CO), f32),
            pltpu.VMEM((ER, EC), f32),
            pltpu.VMEM((ER, EC), f32),
            pltpu.VMEM((RD, CD), f32),
            pltpu.VMEM((1, 128), f32),
            pltpu.VMEM((N_Z, 1, 128), f32),
            pltpu.VMEM((4, 128), f32),
            pltpu.VMEM((N_LANE, 4, 128), f32),
            pltpu.VMEM((N_LANE, 4, 128), f32),
            pltpu.VMEM((N_LANE, 4, 128), f32),
            pltpu.VMEM((4, 128), f32),
            pltpu.VMEM((N_Z, 4, 128), f32),
            pltpu.VMEM((2, 128), f32),
            pltpu.VMEM((N_Z, 2, 128), f32),
            pltpu.VMEM((8, 128), f32),
            pltpu.VMEM((N_LANE, 8, 128), f32),
            pltpu.VMEM((4, 128), f32),
            pltpu.VMEM((N_LANE, 4, 128), f32),
            pltpu.VMEM((16, 8, 128), f32),
            pltpu.VMEM((16, 8, 128), f32),
            pltpu.VMEM((N_LANE, 4, 1, 128), f32),
            pltpu.VMEM((N_GRP * N_TILE, 1, 128), f32),
            pltpu.SemaphoreType.DMA((3,)),
            pltpu.SemaphoreType.DMA((len(DIRECTIONS),)),
            pltpu.SemaphoreType.DMA((len(DIRECTIONS),)),
            pltpu.SemaphoreType.DMA((8,)),
            pltpu.SemaphoreType.DMA((8,)),
            pltpu.SemaphoreType.DMA((HOPS,)),
        ],
        compiler_params=pltpu.CompilerParams(
            collective_id=0, has_side_effects=True, vmem_limit_bytes=55160 * 1024
        ),
    )(right_side, diagonal, inverse_factor)


def solution(mesh):
    placed = (P("grp", "tile"), P("grp", "tile"), P(("grp", "tile"), None))
    return jax.shard_map(
        shards, mesh=mesh, in_specs=placed, out_specs=P("grp", "tile"), check_vma=False
    )
```
